256 devices in a mesh: tile: 32 (over x_hi, z, core), row: 8 (over y, x_lo).
Axes of the slice: x: 4 (x_hi: 2, x_lo: 2; x = x_hi * 2 + x_lo), y: 4, z: 8, core: 2. Of those that a mesh axis runs over, the one named last changes fastest.
Arguments:
- activations: bfloat16 [96, 48, 48, 256], P('tile', 'row'), may hold values from -6 to 6
- matching: int32 [96, 4, 4], replicated, may hold values from 0 to 95, as said below
- first_kernel_weight: bfloat16 [3, 3, 256, 256], replicated, may hold values from -0.125 to 0.125
- conv_second: bfloat16 [3, 3, 256, 256], replicated, may hold values from -0.125 to 0.125
- reduce_kernel_weight: bfloat16 [2, 2, 256, 256], replicated, may hold values from -0.1875 to 0.1875
- cotangent: bfloat16 [96, 24, 24, 256], P('tile', 'row'), may hold values from -6 to 6
Outputs:
- output: bfloat16 [96, 24, 24, 256], P('tile', 'row')
- grad_activations: bfloat16 [96, 48, 48, 256], P('tile', 'row')
- first_kernel_gradient: float32 [3, 3, 256, 256], replicated
- grad_conv_second: float32 [3, 3, 256, 256], replicated
- grad_down: float32 [2, 2, 256, 256], replicated
The draws below stay inside these ranges and needn't reach their ends.
Inputs may be any that keep to these rules, and one draw needn't show every extreme that they name: Entry [t, s] (s = 0 top, 1 bottom, 2 left, 3 right) holds a neighbour tile n, its side s2, a reversal flag f of 0 or 1 and a count q of quarter turns, 0 to 3. The list is a matching of all 384 tile sides: entry [n, s2] holds t, s, the same f and (4 - q) % 4, and no side is matched with itself.
All inputs are finite; a program needn't handle non-finite values.
Results may differ from the reference program's by a relative error of at most 0.013.
Values may be sent and summed in bfloat16 or wider, within the bound.
No kernel may reach another device: no remote copies, remote signals or barrier semaphores. Data moves between devices by JAX's collectives and lax.ppermute only.
A program may use at most 128 MiB of HBM per device.

```python
import math
import jax
import jax.numpy as jnp
from jax import lax

C = 256
NT = 96
TS = 48
HS = 24


def draw_matching(key, part):
    key = jax.random.fold_in(key, 11)
    key_order, key_flip, key_turn = jax.random.split(key, 3)
    edge_count = 4 * NT
    shuffled = jax.random.permutation(key_order, edge_count).astype(jnp.int32)
    first_side = shuffled[0::2]
    second_side = shuffled[1::2]
    reversal = jax.random.randint(key_flip, (edge_count // 2,), 0, 2).astype(jnp.int32)
    quarter = jax.random.randint(key_turn, (edge_count // 2,), 0, 4).astype(jnp.int32)
    blank = jnp.zeros((edge_count,), jnp.int32)
    partner = blank.at[first_side].set(second_side).at[second_side].set(first_side)
    flags = blank.at[first_side].set(reversal).at[second_side].set(reversal)
    turns = blank.at[first_side].set(quarter).at[second_side].set((4 - quarter) % 4)
    entries_table = jnp.stack([partner // 4, partner % 4, flags, turns], axis=1)
    return entries_table.reshape(NT, 4, 4).astype(jnp.int32)


def block_levels(stream_key, extent, cuts, smallest, high):
    def one(dim, shards_of):
        draws = jax.random.uniform(jax.random.fold_in(jax.random.fold_in(stream_key, 6), dim), (shards_of,), jnp.float32, smallest / len(cuts), high / len(cuts))
        return jnp.repeat(jnp.exp(draws), extent[dim] // shards_of).reshape((-1,) + (1,) * (len(extent) - dim - 1))

    level = one(*cuts[0])
    for cut in cuts[1:]:
        level = level * one(*cut)
    return level


def bell_draw(own_key, dims, spread, bound, cuts=(), held_as=jnp.bfloat16):
    array = spread * jax.random.normal(own_key, dims, jnp.float32)
    if cuts:
        array = array * block_levels(own_key, dims, cuts, -0.22, 0.18)
    return jnp.clip(array, -bound, bound).astype(held_as)


def setup_inputs(seed: int = 0) -> dict:
    seeds = jax.random.split(jax.random.key(seed), 7)
    return {
        "activations": bell_draw(seeds[0], (NT, TS, TS, C), 1.0, 6.0, ((0, 32), (1, 8))),
        "matching": draw_matching(jax.random.fold_in(seeds[6], 71), 0),
        "first_kernel_weight": bell_draw(seeds[2], (3, 3, C, C), (9 * C) ** -0.5, 0.125),
        "conv_second": bell_draw(seeds[3], (3, 3, C, C), (9 * C) ** -0.5, 0.125),
        "reduce_kernel_weight": bell_draw(seeds[4], (2, 2, C, C), (4 * C) ** -0.5, 0.1875),
        "cotangent": bell_draw(seeds[5], (NT, HS, HS, C), 1.0, 6.0, ((0, 32), (1, 8))),
    }


def edge_rows(sphere_signal):
    return jnp.stack([sphere_signal[:, 0], sphere_signal[:, -1], sphere_signal[:, :, 0], sphere_signal[:, :, -1]], axis=1)

def turn_lines(edge_lines, reversal, quarter):
    flipped = jnp.where((reversal == 1)[..., None, None], jnp.flip(edge_lines, axis=-2), edge_lines)
    half_width = edge_lines.shape[-1] // 2
    first_half = flipped[..., :half_width].astype(jnp.float32)
    second_half = flipped[..., half_width:].astype(jnp.float32)
    cosine = jnp.where(quarter == 0, 1.0, jnp.where(quarter == 2, -1.0, 0.0)).astype(jnp.float32)[..., None, None]
    sine_part = jnp.where(quarter == 1, 1.0, jnp.where(quarter == 3, -1.0, 0.0)).astype(jnp.float32)[..., None, None]
    turned = jnp.concatenate([cosine * first_half - sine_part * second_half, sine_part * first_half + cosine * second_half], axis=-1)
    return turned.astype(edge_lines.dtype)

def padded_tiles(sphere_signal, matching):
    picked = edge_rows(sphere_signal)[matching[..., 0], matching[..., 1]]
    ghosts = turn_lines(picked, matching[..., 2], matching[..., 3])
    padded = jnp.pad(sphere_signal, ((0, 0), (1, 1), (1, 1), (0, 0)))
    padded = padded.at[:, 0, 1:-1].set(ghosts[:, 0]).at[:, -1, 1:-1].set(ghosts[:, 1])
    padded = padded.at[:, 1:-1, 0].set(ghosts[:, 2]).at[:, 1:-1, -1].set(ghosts[:, 3])
    return padded

def unpad_tiles(padded_grad, matching):
    border = jnp.stack([padded_grad[:, 0, 1:-1], padded_grad[:, -1, 1:-1], padded_grad[:, 1:-1, 0], padded_grad[:, 1:-1, -1]], axis=1)
    routed = turn_lines(border[matching[..., 0], matching[..., 1]], matching[..., 2], matching[..., 3])
    interior = padded_grad[:, 1:-1, 1:-1]
    interior = interior.at[:, 0].add(routed[:, 0]).at[:, -1].add(routed[:, 1])
    interior = interior.at[:, :, 0].add(routed[:, 2]).at[:, :, -1].add(routed[:, 3])
    return interior

def convolve(padded, kernel_weight):
    rows = padded.shape[1] - 2
    columns = padded.shape[2] - 2
    total = jnp.zeros((padded.shape[0], rows, columns, kernel_weight.shape[3]), jnp.float32)
    for row_tap in range(3):
        for col_tap in range(3):
            total = total + jnp.dot(padded[:, row_tap:row_tap + rows, col_tap:col_tap + columns], kernel_weight[row_tap, col_tap], preferred_element_type=jnp.float32)
    return total

def convolve_back(grads, kernel_weight):
    rows = grads.shape[1]
    columns = grads.shape[2]
    total = jnp.zeros((grads.shape[0], rows + 2, columns + 2, kernel_weight.shape[2]), jnp.float32)
    for row_tap in range(3):
        for col_tap in range(3):
            term = lax.dot_general(grads, kernel_weight[row_tap, col_tap], (((3,), (1,)), ((), ())), preferred_element_type=jnp.float32)
            total = total.at[:, row_tap:row_tap + rows, col_tap:col_tap + columns].add(term)
    return total

def weight_grad(padded, grads):
    rows = grads.shape[1]
    columns = grads.shape[2]
    result = []
    for row_tap in range(3):
        line_terms = []
        for col_tap in range(3):
            line_terms.append(lax.dot_general(padded[:, row_tap:row_tap + rows, col_tap:col_tap + columns], grads, (((0, 1, 2), (0, 1, 2)), ((), ())), preferred_element_type=jnp.float32))
        result.append(jnp.stack(line_terms, axis=0))
    return jnp.stack(result, axis=0)

def grouped_cells(sphere_signal):
    tiles, rows, columns, chans = sphere_signal.shape
    return sphere_signal.reshape(tiles, rows // 2, 2, columns // 2, 2, chans)

def strided_shrink(sphere_signal, kernel_weight):
    grouped = grouped_cells(sphere_signal)
    total = jnp.zeros((sphere_signal.shape[0], sphere_signal.shape[1] // 2, sphere_signal.shape[2] // 2, kernel_weight.shape[3]), jnp.float32)
    for row_tap in range(2):
        for col_tap in range(2):
            total = total + jnp.dot(grouped[:, :, row_tap, :, col_tap], kernel_weight[row_tap, col_tap], preferred_element_type=jnp.float32)
    return total

def upsample_back(grads, kernel_weight):
    tiles, rows, columns, chans = grads.shape
    stacked = []
    for row_tap in range(2):
        pieces = [lax.dot_general(grads, kernel_weight[row_tap, col_tap], (((3,), (1,)), ((), ())), preferred_element_type=jnp.float32) for col_tap in range(2)]
        stacked.append(jnp.stack(pieces, axis=3))
    return jnp.stack(stacked, axis=2).reshape(tiles, rows * 2, columns * 2, kernel_weight.shape[2])

def down_grad(sphere_signal, grads):
    grouped = grouped_cells(sphere_signal)
    result = []
    for row_tap in range(2):
        pieces = [lax.dot_general(grouped[:, :, row_tap, :, col_tap], grads, (((0, 1, 2), (0, 1, 2)), ((), ())), preferred_element_type=jnp.float32) for col_tap in range(2)]
        result.append(jnp.stack(pieces, axis=0))
    return jnp.stack(result, axis=0)

def silu(value):
    return value * jax.nn.sigmoid(value)

def silu_slope(value):
    sigma = jax.nn.sigmoid(value)
    return sigma * (1.0 + value * (1.0 - sigma))

def reference(activations, matching, first_kernel_weight, conv_second, reduce_kernel_weight, cotangent):
    norm_factor = 1.0 / math.sqrt(NT * TS * TS)
    padded_input = padded_tiles(activations, matching)
    pre_first = convolve(padded_input, first_kernel_weight)
    hidden_first = silu(pre_first).astype(jnp.bfloat16)
    padded_hidden = padded_tiles(hidden_first, matching)
    pre_second = convolve(padded_hidden, conv_second)
    second_hidden_state = silu(pre_second).astype(jnp.bfloat16)
    output = strided_shrink(second_hidden_state, reduce_kernel_weight).astype(jnp.bfloat16)
    grad_second = (upsample_back(cotangent, reduce_kernel_weight) * silu_slope(pre_second)).astype(jnp.bfloat16)
    grad_first_hidden = unpad_tiles(convolve_back(grad_second, conv_second), matching)
    grad_first = (grad_first_hidden * silu_slope(pre_first)).astype(jnp.bfloat16)
    grad_activations = unpad_tiles(convolve_back(grad_first, first_kernel_weight), matching).astype(jnp.bfloat16)
    first_kernel_gradient = weight_grad(padded_input, grad_first) * norm_factor
    grad_conv_second = weight_grad(padded_hidden, grad_second) * norm_factor
    grad_down = down_grad(second_hidden_state, cotangent) * norm_factor
    return (output, grad_activations, first_kernel_gradient, grad_conv_second, grad_down)
```

```python
import math

import jax
import jax.numpy as jnp
from jax import lax
from jax.sharding import Mesh, PartitionSpec as P

XH, Z, CORE, Y, XL = 2, 8, 2, 4, 2
ROWS = Y * XL
TILE_AXES = ("xh", "z", "c")
ROW_AXES = ("y", "xl")
COLUMN_AXES = ("xh", "c")
f32 = jnp.float32
bf16 = jnp.bfloat16


def broadcast_all(piece, axes, count):
    return lax.all_to_all(
        jnp.broadcast_to(piece[None], (count,) + piece.shape), axes, 0, 0, tiled=True
    )


def routing(matching):
    tiles = matching.shape[0]
    here = tiles // (XH * Z * CORE)
    lines = here * 4
    xh, z, core = lax.axis_index("xh"), lax.axis_index("z"), lax.axis_index("c")
    grouped = matching.reshape(XH, Z, CORE, lines, 4)
    column = lax.dynamic_index_in_dim(grouped, z, 1, keepdims=False).reshape(XH * CORE * lines, 4)
    group = column[:, 0] // here
    held = (group // (Z * CORE) == xh) & (group % CORE == core)
    place = ((group // CORE) % Z) * lines + (column[:, 0] % here) * 4 + column[:, 1]
    pick = held[:, None] & (place[:, None] == jnp.arange(Z * lines)[None, :])
    mine = lax.dynamic_slice_in_dim(column, (xh * CORE + core) * lines, lines, 0)
    my_group = mine[:, 0] // here
    source = (my_group // (Z * CORE)) * CORE + my_group % CORE
    return {
        "pick": pick.astype(bf16),
        "from": source[None, :] == jnp.arange(XH * CORE)[:, None],
        "flip": mine[:, 2] == 1,
        "quarter": mine[:, 3],
        "row": lax.axis_index(ROW_AXES),
    }


def turn_channels(lines, quarter):
    half = lines.shape[-1] // 2
    first, second = lines[..., :half], lines[..., half:]
    quarter = quarter[:, None, None]
    odd = quarter % 2 == 1
    lead = jnp.where(odd, second, first)
    trail = jnp.where(odd, first, second)
    lead = jnp.where((quarter == 1) | (quarter == 2), -lead, lead)
    trail = jnp.where((quarter == 2) | (quarter == 3), -trail, trail)
    return jnp.concatenate([lead, trail], axis=-1)


def exchange(top, bottom, left, right, plan):
    tiles, width, channels = top.shape
    strip = width // ROWS
    ends = jnp.where(plan["row"] == ROWS - 1, bottom, top)
    ends = ends.reshape(tiles, ROWS, strip, channels).transpose(1, 0, 2, 3)
    ends = lax.all_to_all(ends, ROW_AXES, 0, 0, tiled=True)
    pieces = jnp.stack([ends[0], ends[ROWS - 1], left, right], axis=1)
    lines = tiles * 4
    pieces = pieces.reshape(lines, strip * channels)
    gathered = broadcast_all(pieces, "z", Z).reshape(Z * lines, strip * channels)
    chosen = jnp.dot(plan["pick"], gathered, preferred_element_type=f32).astype(bf16)
    arrived = lax.all_to_all(
        chosen.reshape(XH * CORE, lines, strip * channels), COLUMN_AXES, 0, 0, tiled=True
    )
    mine = jnp.where(plan["from"][0][:, None], arrived[0], arrived[1])
    mine = jnp.where(plan["from"][2][:, None], arrived[2], mine)
    mine = jnp.where(plan["from"][3][:, None], arrived[3], mine)
    mine = turn_channels(mine.reshape(lines, strip, channels), plan["quarter"])
    mine = jnp.where(plan["flip"][:, None, None], mine[:, ::-1], mine)
    whole = broadcast_all(mine, ROW_AXES, ROWS)
    whole = jnp.where(plan["flip"][None, :, None, None], whole[::-1], whole)
    return whole.transpose(1, 0, 2, 3).reshape(tiles, 4, width, channels)


def own_part(lines, margin, plan):
    strip = lines.shape[1] // ROWS
    padded = jnp.pad(lines, ((0, 0), (margin, margin), (0, 0)))
    return lax.dynamic_slice_in_dim(padded, plan["row"] * strip, strip + 2 * margin, 1)


def with_ghosts(strips, ghosts, margin, plan):
    row = plan["row"]
    above = jnp.where(row == 0, ghosts[:, 0], strips[:, margin - 1])
    below = jnp.where(row == ROWS - 1, ghosts[:, 1], strips[:, -margin])
    middle = jnp.concatenate(
        [strips[:, : margin - 1], above[:, None], strips[:, margin:-margin], below[:, None]]
        + ([strips[:, -margin + 1 :]] if margin > 1 else []),
        axis=1,
    )
    left = own_part(ghosts[:, 2], margin, plan)
    right = own_part(ghosts[:, 3], margin, plan)
    return jnp.concatenate([left[:, :, None], middle, right[:, :, None]], axis=2)


def add_borders(interior, routed, margin, plan):
    row = plan["row"]
    routed = routed.astype(f32)
    rows = interior.shape[1]
    index = jnp.arange(rows)[None, :, None, None]
    top = jnp.where((row == 0) & (index == margin), routed[:, 0][:, None], 0.0)
    bottom = jnp.where(
        (row == ROWS - 1) & (index == rows - 1 - margin), routed[:, 1][:, None], 0.0
    )
    column = jnp.arange(interior.shape[2])[None, None, :, None]
    left = own_part(routed[:, 2], margin, plan)[:, :, None]
    right = own_part(routed[:, 3], margin, plan)[:, :, None]
    sides = jnp.where(column == 0, left, 0.0) + jnp.where(
        column == interior.shape[2] - 1, right, 0.0
    )
    return interior + top + bottom + sides


def inside(rows, margin, width, plan):
    strip = width // ROWS
    place = plan["row"] * strip - margin + jnp.arange(rows)
    return ((place >= 0) & (place < width))[None, :, None, None]


def convolve(padded, kernel_weight):
    rows = padded.shape[1] - 2
    columns = padded.shape[2] - 2
    total = None
    for row_tap in range(3):
        for col_tap in range(3):
            term = jnp.dot(
                padded[:, row_tap : row_tap + rows, col_tap : col_tap + columns],
                kernel_weight[row_tap, col_tap],
                preferred_element_type=f32,
            )
            total = term if total is None else total + term
    return total


def convolve_back(grads, kernel_weight):
    rows = grads.shape[1] - 2
    columns = grads.shape[2]
    grads = jnp.pad(grads, ((0, 0), (0, 0), (2, 2), (0, 0)))
    total = None
    for row_tap in range(3):
        for col_tap in range(3):
            term = lax.dot_general(
                grads[:, row_tap : row_tap + rows, col_tap : col_tap + columns + 2],
                kernel_weight[2 - row_tap, 2 - col_tap],
                (((3,), (1,)), ((), ())),
                preferred_element_type=f32,
            )
            total = term if total is None else total + term
    return total


def weight_grad(padded, grads):
    rows = grads.shape[1]
    columns = grads.shape[2]
    return [
        lax.dot_general(
            padded[:, row_tap : row_tap + rows, col_tap : col_tap + columns],
            grads,
            (((0, 1, 2), (0, 1, 2)), ((), ())),
            preferred_element_type=f32,
        )
        for row_tap in range(3)
        for col_tap in range(3)
    ]


def grouped_cells(field):
    tiles, rows, columns, channels = field.shape
    return field.reshape(tiles, rows // 2, 2, columns // 2, 2, channels)


def strided_shrink(field, kernel_weight):
    grouped = grouped_cells(field)
    total = None
    for row_tap in range(2):
        for col_tap in range(2):
            term = jnp.dot(
                grouped[:, :, row_tap, :, col_tap],
                kernel_weight[row_tap, col_tap],
                preferred_element_type=f32,
            )
            total = term if total is None else total + term
    return total


def upsample_back(grads, kernel_weight):
    tiles, rows, columns, channels = grads.shape
    stacked = []
    for row_tap in range(2):
        pieces = [
            lax.dot_general(
                grads,
                kernel_weight[row_tap, col_tap],
                (((3,), (1,)), ((), ())),
                preferred_element_type=f32,
            )
            for col_tap in range(2)
        ]
        stacked.append(jnp.stack(pieces, axis=3))
    return jnp.stack(stacked, axis=2).reshape(tiles, rows * 2, columns * 2, kernel_weight.shape[2])


def down_grad(field, grads):
    grouped = grouped_cells(field)
    return [
        lax.dot_general(
            grouped[:, :, row_tap, :, col_tap],
            grads,
            (((0, 1, 2), (0, 1, 2)), ((), ())),
            preferred_element_type=f32,
        )
        for row_tap in range(2)
        for col_tap in range(2)
    ]


def silu(value):
    return value * jax.nn.sigmoid(value)


def silu_slope(value):
    sigma = jax.nn.sigmoid(value)
    return sigma * (1.0 + value * (1.0 - sigma))


def sum_everywhere(blocks, factor):
    channels = blocks[0].shape[-1]
    count = len(blocks)
    half = count // 2
    core = lax.axis_index("c")
    first = jnp.concatenate(blocks[:half], axis=0)
    second = jnp.concatenate(blocks[half:], axis=0)
    swap = [(0, 1), (1, 0)]
    sent = jnp.where(core == 0, second, first).astype(bf16)
    held = jnp.where(core == 0, first, second) + lax.ppermute(sent, "c", swap).astype(f32)
    held = held.astype(bf16).reshape(ROWS, -1, channels)
    held = lax.all_to_all(held, ROW_AXES, 0, 0, tiled=True).astype(f32).sum(0)
    held = held.astype(bf16).reshape(XH * Z, -1, channels)
    held = lax.all_to_all(held, ("xh", "z"), 0, 0, tiled=True).astype(f32).sum(0)
    held = (held * factor).astype(bf16)
    held = broadcast_all(held, ("xh", "z"), XH * Z).reshape(-1, channels)
    held = broadcast_all(held, ROW_AXES, ROWS).reshape(-1, channels)
    other = lax.ppermute(held, "c", swap)
    first = jnp.where(core == 0, held, other)
    second = jnp.where(core == 0, other, held)
    both = jnp.concatenate([first, second], axis=0).astype(f32)
    return both.reshape(count, channels, channels)


def body(activations, matching, first_kernel_weight, conv_second, reduce_kernel_weight, cotangent):
    tiles, strip, width, channels = activations.shape
    plan = routing(matching)
    factor = 1.0 / math.sqrt(matching.shape[0] * width * width)

    first_rows = jnp.concatenate(
        [activations[:, :4].reshape(tiles, 4 * width, channels), cotangent[:, 0]], axis=1
    )
    last_rows = jnp.concatenate(
        [activations[:, -4:].reshape(tiles, 4 * width, channels), cotangent[:, -1]], axis=1
    )
    above = lax.ppermute(last_rows, ROW_AXES, [(i, i + 1) for i in range(ROWS - 1)])
    below = lax.ppermute(first_rows, ROW_AXES, [(i + 1, i) for i in range(ROWS - 1)])
    cells = 4 * width
    wide_input = jnp.concatenate(
        [
            above[:, :cells].reshape(tiles, 4, width, channels),
            activations,
            below[:, :cells].reshape(tiles, 4, width, channels),
        ],
        axis=1,
    )
    wide_cotangent = jnp.concatenate(
        [above[:, None, cells:], cotangent, below[:, None, cells:]], axis=1
    )

    ghosts = exchange(
        activations[:, 0], activations[:, -1], activations[:, :, 0], activations[:, :, -1], plan
    )
    padded_input = with_ghosts(wide_input, ghosts, 4, plan)
    pre_first = convolve(padded_input, first_kernel_weight)
    hidden_first = jnp.where(
        inside(strip + 6, 3, width, plan), silu(pre_first).astype(bf16), jnp.zeros((), bf16)
    )

    ghosts = exchange(
        hidden_first[:, 3],
        hidden_first[:, -4],
        hidden_first[:, 3:-3, 0],
        hidden_first[:, 3:-3, -1],
        plan,
    )
    padded_hidden = with_ghosts(hidden_first, ghosts, 3, plan)
    pre_second = convolve(padded_hidden, conv_second)
    hidden_second = silu(pre_second[:, 2:-2]).astype(bf16)
    output = strided_shrink(hidden_second, reduce_kernel_weight).astype(bf16)
    grad_second = (
        upsample_back(wide_cotangent, reduce_kernel_weight) * silu_slope(pre_second)
    ).astype(bf16)

    spread = convolve_back(grad_second, conv_second)
    routed = exchange(
        spread[:, 0, 1:-1].astype(bf16),
        spread[:, -1, 1:-1].astype(bf16),
        spread[:, 1:-1, 0].astype(bf16),
        spread[:, 1:-1, -1].astype(bf16),
        plan,
    )
    grad_first_hidden = add_borders(spread[:, :, 1:-1], routed, 1, plan)
    grad_first = jnp.where(
        inside(strip + 2, 1, width, plan),
        (grad_first_hidden * silu_slope(pre_first[:, 2:-2])).astype(bf16),
        jnp.zeros((), bf16),
    )

    spread = convolve_back(jnp.pad(grad_first, ((0, 0), (1, 1), (0, 0), (0, 0))), first_kernel_weight)
    routed = exchange(
        spread[:, 0, 1:-1].astype(bf16),
        spread[:, -1, 1:-1].astype(bf16),
        spread[:, 1:-1, 0].astype(bf16),
        spread[:, 1:-1, -1].astype(bf16),
        plan,
    )
    grad_activations = add_borders(spread[:, 1:-1, 1:-1], routed, 0, plan).astype(bf16)

    summed = sum_everywhere(
        weight_grad(padded_input[:, 3:-3], grad_first[:, 1:-1])
        + weight_grad(padded_hidden[:, 2:-2], grad_second[:, 2:-2])
        + down_grad(hidden_second, cotangent),
        factor,
    )
    square = (channels, channels)
    return (
        output,
        grad_activations,
        summed[:9].reshape((3, 3) + square),
        summed[9:18].reshape((3, 3) + square),
        summed[18:].reshape((2, 2) + square),
    )


def solution(mesh):
    fine = Mesh(mesh.devices.reshape(XH, Z, CORE, Y, XL), TILE_AXES + ROW_AXES)
    placed = P(TILE_AXES, ROW_AXES, None, None)
    return jax.shard_map(
        body,
        mesh=fine,
        in_specs=(placed, P(), P(), P(), P(), placed),
        out_specs=(placed, placed, P(), P(), P()),
        check_vma=False,
    )
```

```python
import math

import jax
import jax.numpy as jnp
from jax import lax
from jax.sharding import Mesh, PartitionSpec as P

XH, Z, CORE, Y, XL = 2, 8, 2, 4, 2
ROWS = Y * XL
TILE_AXES = ("xh", "z", "c")
ROW_AXES = ("y", "xl")
COLUMN_AXES = ("xh", "c")
f32 = jnp.float32
bf16 = jnp.bfloat16


def broadcast_all(piece, axes, count):
    return lax.all_to_all(
        jnp.broadcast_to(piece[None], (count,) + piece.shape), axes, 0, 0, tiled=True
    )


def column_of(group):
    return (group // (Z * CORE)) * CORE + group % CORE


def routing(matching):
    tiles = matching.shape[0]
    here = tiles // (XH * Z * CORE)
    lines = here * 4
    xh, z, core = lax.axis_index("xh"), lax.axis_index("z"), lax.axis_index("c")
    me = xh * CORE + core
    sides = matching.reshape(tiles * 4, 4)
    grouped = matching.reshape(XH, Z, CORE, lines, 4)
    column = lax.dynamic_index_in_dim(grouped, z, 1, keepdims=False).reshape(XH * CORE * lines, 4)
    tile, side = column[:, 0], column[:, 1]
    beside = jnp.where(side < 2, 2, 0)[:, None] + jnp.arange(2)[None, :]
    corners = sides[tile[:, None] * 4 + beside]
    finish = (side[:, None] % 2) ^ corners[..., 2]

    def choice(tile, side):
        group = tile // here
        place = ((group // CORE) % Z) * lines + (tile % here) * 4 + side
        held = column_of(group) == me
        return (held[..., None] & (place[..., None] == jnp.arange(Z * lines))).astype(bf16)

    def own(table):
        return lax.dynamic_slice_in_dim(table, me * lines, lines, 0)

    mine, my_corners = own(column), own(corners)
    return {
        "pick": choice(tile, side),
        "pick_corner": choice(corners[..., 0], corners[..., 1]).reshape(-1, Z * lines),
        "from": column_of(mine[:, 0] // here),
        "from_corner": column_of(my_corners[..., 0] // here),
        "side": mine[:, 1],
        "flip": mine[:, 2] == 1,
        "quarter": mine[:, 3],
        "quarter_corner": my_corners[..., 3],
        "finish": own(finish) == 1,
        "row": lax.axis_index(ROW_AXES),
    }


def turn_channels(lines, quarter):
    half = lines.shape[-1] // 2
    first, second = lines[..., :half], lines[..., half:]
    quarter = quarter.reshape(quarter.shape + (1,) * (lines.ndim - quarter.ndim))
    odd = quarter % 2 == 1
    lead = jnp.where(odd, second, first)
    trail = jnp.where(odd, first, second)
    lead = jnp.where((quarter == 1) | (quarter == 2), -lead, lead)
    trail = jnp.where((quarter == 2) | (quarter == 3), -trail, trail)
    return jnp.concatenate([lead, trail], axis=-1)


def flip_lines(lines, flip):
    return jnp.where(flip[:, None, None], lines[:, ::-1], lines)


def to_here(lines, plan):
    return turn_channels(flip_lines(lines, plan["flip"]), plan["quarter"])


def to_neighbour(lines, plan):
    return turn_channels(flip_lines(lines, plan["flip"]), (4 - plan["quarter"]) % 4)


def from_columns(arrived, source):
    source = source.reshape(source.shape + (1,) * (arrived.ndim - 1 - source.ndim))
    result = arrived[0]
    for column in range(1, XH * CORE):
        result = jnp.where(source == column, arrived[column], result)
    return result


def exchange(top, bottom, left, right, plan):
    tiles, units, width, channels = top.shape
    strip = width // ROWS
    lines = tiles * 4
    ends = jnp.where(plan["row"] == ROWS - 1, bottom, top)
    ends = ends.reshape(tiles, units, ROWS, strip, channels).transpose(2, 0, 1, 3, 4)
    ends = lax.all_to_all(ends, ROW_AXES, 0, 0, tiled=True)
    pieces = jnp.stack([ends[0], ends[ROWS - 1], left, right], axis=1)
    long = units * strip * channels
    pieces = pieces.reshape(lines, long)
    gathered = broadcast_all(pieces, "z", Z).reshape(Z * lines, long)
    cells = gathered[:, : strip * channels]
    near = 2 * channels
    head = cells[:, :near]
    tail = jnp.concatenate([cells[:, -channels:], cells[:, -near:-channels]], axis=1)
    corner = jnp.where(plan["row"] == 0, head, tail)
    chosen = jnp.dot(plan["pick"], gathered, preferred_element_type=f32).astype(bf16)
    corner = jnp.dot(plan["pick_corner"], corner, preferred_element_type=f32).astype(bf16)
    columns = XH * CORE
    sent = jnp.concatenate(
        [chosen.reshape(columns, lines, long), corner.reshape(columns, lines, 2 * near)], axis=2
    )
    arrived = lax.all_to_all(sent, COLUMN_AXES, 0, 0, tiled=True)
    corner = arrived[:, :, long:].reshape(columns, lines, 2, near)
    mine = jnp.concatenate(
        [
            from_columns(arrived[:, :, :long], plan["from"]),
            from_columns(corner, plan["from_corner"]).reshape(lines, 2 * near),
            pieces[:, : strip * channels],
        ],
        axis=1,
    )
    whole = broadcast_all(mine, ROW_AXES, ROWS)
    theirs = whole[:, :, :long].reshape(ROWS, lines, units, strip, channels)
    theirs = theirs.transpose(1, 2, 0, 3, 4).reshape(lines, units, width, channels)
    own = whole[:, :, long + 2 * near :].reshape(ROWS, lines, strip, channels)
    own = own.transpose(1, 0, 2, 3).reshape(lines, width, channels)
    corner = whole[:, :, long : long + 2 * near].reshape(ROWS, lines, 2, 2, channels)
    corner = jnp.where(plan["finish"][:, :, None, None], corner[ROWS - 1], corner[0])
    corner = turn_channels(corner, plan["quarter_corner"])
    return theirs, own, corner


def by_side(cells, plan):
    blocks = [
        jnp.where((plan["side"] == side)[:, None, None], cells, jnp.zeros((), cells.dtype))
        for side in range(4)
    ]
    return jnp.concatenate(blocks, axis=-1)


def neighbour_edge(theirs, own, corner, kernel_weight, plan):
    width = own.shape[1]
    w = kernel_weight
    patch = [
        jnp.pad(to_neighbour(own, plan), ((0, 0), (1, 1), (0, 0))),
        jnp.concatenate([corner[:, 0, :1], theirs[:, 0], corner[:, 1, :1]], axis=1),
        jnp.concatenate([corner[:, 0, 1:], theirs[:, 1], corner[:, 1, 1:]], axis=1),
    ]
    total = None
    for depth in range(3):
        spread = by_side(patch[depth], plan)
        for tap in range(3):
            weights = jnp.concatenate(
                [w[depth, tap], w[2 - depth, tap], w[tap, depth], w[tap, 2 - depth]], axis=0
            )
            term = jnp.dot(spread[:, tap : tap + width], weights, preferred_element_type=f32)
            total = term if total is None else total + term
    return total


def neighbour_border(grads, kernel_weight, plan):
    width = grads.shape[1]
    w = kernel_weight
    spread = by_side(jnp.pad(grads, ((0, 0), (1, 1), (0, 0))), plan)
    total = None
    for tap in range(3):
        weights = jnp.concatenate(
            [w[0, 2 - tap], w[2, 2 - tap], w[2 - tap, 0], w[2 - tap, 2]], axis=1
        )
        term = lax.dot_general(
            spread[:, tap : tap + width],
            weights,
            (((2,), (1,)), ((), ())),
            preferred_element_type=f32,
        )
        total = term if total is None else total + term
    return total


def own_part(lines, margin, plan):
    strip = lines.shape[1] // ROWS
    padded = jnp.pad(lines, ((0, 0), (margin, margin), (0, 0)))
    return lax.dynamic_slice_in_dim(padded, plan["row"] * strip, strip + 2 * margin, 1)


def with_ghosts(strips, ghosts, margin, plan):
    row = plan["row"]
    above = jnp.where(row == 0, ghosts[:, 0], strips[:, margin - 1])
    below = jnp.where(row == ROWS - 1, ghosts[:, 1], strips[:, -margin])
    middle = jnp.concatenate(
        [strips[:, : margin - 1], above[:, None], strips[:, margin:-margin], below[:, None]]
        + ([strips[:, -margin + 1 :]] if margin > 1 else []),
        axis=1,
    )
    left = own_part(ghosts[:, 2], margin, plan)
    right = own_part(ghosts[:, 3], margin, plan)
    return jnp.concatenate([left[:, :, None], middle, right[:, :, None]], axis=2)


def add_borders(interior, routed, margin, plan):
    row = plan["row"]
    routed = routed.astype(f32)
    rows = interior.shape[1]
    index = jnp.arange(rows)[None, :, None, None]
    top = jnp.where((row == 0) & (index == margin), routed[:, 0][:, None], 0.0)
    bottom = jnp.where(
        (row == ROWS - 1) & (index == rows - 1 - margin), routed[:, 1][:, None], 0.0
    )
    column = jnp.arange(interior.shape[2])[None, None, :, None]
    left = own_part(routed[:, 2], margin, plan)[:, :, None]
    right = own_part(routed[:, 3], margin, plan)[:, :, None]
    sides = jnp.where(column == 0, left, 0.0) + jnp.where(
        column == interior.shape[2] - 1, right, 0.0
    )
    return interior + top + bottom + sides


def inside(rows, margin, width, plan):
    strip = width // ROWS
    place = plan["row"] * strip - margin + jnp.arange(rows)
    return ((place >= 0) & (place < width))[None, :, None, None]


def convolve(padded, kernel_weight):
    rows = padded.shape[1] - 2
    columns = padded.shape[2] - 2
    total = None
    for row_tap in range(3):
        for col_tap in range(3):
            term = jnp.dot(
                padded[:, row_tap : row_tap + rows, col_tap : col_tap + columns],
                kernel_weight[row_tap, col_tap],
                preferred_element_type=f32,
            )
            total = term if total is None else total + term
    return total


def convolve_back(grads, kernel_weight):
    rows = grads.shape[1] - 2
    columns = grads.shape[2]
    grads = jnp.pad(grads, ((0, 0), (0, 0), (2, 2), (0, 0)))
    total = None
    for row_tap in range(3):
        for col_tap in range(3):
            term = lax.dot_general(
                grads[:, row_tap : row_tap + rows, col_tap : col_tap + columns + 2],
                kernel_weight[2 - row_tap, 2 - col_tap],
                (((3,), (1,)), ((), ())),
                preferred_element_type=f32,
            )
            total = term if total is None else total + term
    return total


def weight_grad(padded, grads):
    rows = grads.shape[1]
    columns = grads.shape[2]
    return [
        lax.dot_general(
            padded[:, row_tap : row_tap + rows, col_tap : col_tap + columns],
            grads,
            (((0, 1, 2), (0, 1, 2)), ((), ())),
            preferred_element_type=f32,
        )
        for row_tap in range(3)
        for col_tap in range(3)
    ]


def grouped_cells(field):
    tiles, rows, columns, channels = field.shape
    return field.reshape(tiles, rows // 2, 2, columns // 2, 2, channels)


def strided_shrink(field, kernel_weight):
    grouped = grouped_cells(field)
    total = None
    for row_tap in range(2):
        for col_tap in range(2):
            term = jnp.dot(
                grouped[:, :, row_tap, :, col_tap],
                kernel_weight[row_tap, col_tap],
                preferred_element_type=f32,
            )
            total = term if total is None else total + term
    return total


def upsample_back(grads, kernel_weight):
    tiles, rows, columns, channels = grads.shape
    stacked = []
    for row_tap in range(2):
        pieces = [
            lax.dot_general(
                grads,
                kernel_weight[row_tap, col_tap],
                (((3,), (1,)), ((), ())),
                preferred_element_type=f32,
            )
            for col_tap in range(2)
        ]
        stacked.append(jnp.stack(pieces, axis=3))
    return jnp.stack(stacked, axis=2).reshape(tiles, rows * 2, columns * 2, kernel_weight.shape[2])


def down_grad(field, grads):
    grouped = grouped_cells(field)
    return [
        lax.dot_general(
            grouped[:, :, row_tap, :, col_tap],
            grads,
            (((0, 1, 2), (0, 1, 2)), ((), ())),
            preferred_element_type=f32,
        )
        for row_tap in range(2)
        for col_tap in range(2)
    ]


def silu(value):
    return value * jax.nn.sigmoid(value)


def silu_slope(value):
    sigma = jax.nn.sigmoid(value)
    return sigma * (1.0 + value * (1.0 - sigma))


def sum_everywhere(blocks, factor):
    channels = blocks[0].shape[-1]
    count = len(blocks)
    half = count // 2
    core = lax.axis_index("c")
    first = jnp.concatenate(blocks[:half], axis=0)
    second = jnp.concatenate(blocks[half:], axis=0)
    swap = [(0, 1), (1, 0)]
    sent = jnp.where(core == 0, second, first).astype(bf16)
    held = jnp.where(core == 0, first, second) + lax.ppermute(sent, "c", swap).astype(f32)
    held = held.astype(bf16).reshape(ROWS, -1, channels)
    held = lax.all_to_all(held, ROW_AXES, 0, 0, tiled=True).astype(f32).sum(0)
    held = held.astype(bf16).reshape(XH * Z, -1, channels)
    held = lax.all_to_all(held, ("xh", "z"), 0, 0, tiled=True).astype(f32).sum(0)
    held = (held * factor).astype(bf16)
    held = broadcast_all(held, ("xh", "z"), XH * Z).reshape(-1, channels)
    held = broadcast_all(held, ROW_AXES, ROWS).reshape(-1, channels)
    other = lax.ppermute(held, "c", swap)
    first = jnp.where(core == 0, held, other)
    second = jnp.where(core == 0, other, held)
    both = jnp.concatenate([first, second], axis=0).astype(f32)
    return both.reshape(count, channels, channels)


def body(activations, matching, first_kernel_weight, conv_second, reduce_kernel_weight, cotangent):
    tiles, strip, width, channels = activations.shape
    plan = routing(matching)
    factor = 1.0 / math.sqrt(matching.shape[0] * width * width)

    first_rows = jnp.concatenate(
        [activations[:, :4].reshape(tiles, 4 * width, channels), cotangent[:, 0]], axis=1
    )
    last_rows = jnp.concatenate(
        [activations[:, -4:].reshape(tiles, 4 * width, channels), cotangent[:, -1]], axis=1
    )
    above = lax.ppermute(last_rows, ROW_AXES, [(i, i + 1) for i in range(ROWS - 1)])
    below = lax.ppermute(first_rows, ROW_AXES, [(i + 1, i) for i in range(ROWS - 1)])
    cells = 4 * width
    wide_input = jnp.concatenate(
        [
            above[:, :cells].reshape(tiles, 4, width, channels),
            activations,
            below[:, :cells].reshape(tiles, 4, width, channels),
        ],
        axis=1,
    )
    wide_cotangent = jnp.concatenate(
        [above[:, None, cells:], cotangent, below[:, None, cells:]], axis=1
    )

    def sides_of(lines):
        return lines.reshape(tiles, 4, width, channels)

    theirs, own, corner = exchange(
        activations[:, :2],
        activations[:, :-3:-1],
        activations[:, :, :2].swapaxes(1, 2),
        activations[:, :, :-3:-1].swapaxes(1, 2),
        plan,
    )
    edge_first = neighbour_edge(theirs, own, corner, first_kernel_weight, plan)
    ghosts = sides_of(to_here(theirs[:, 0], plan))
    padded_input = with_ghosts(wide_input, ghosts, 4, plan)
    pre_first = convolve(padded_input, first_kernel_weight)
    hidden_first = jnp.where(
        inside(strip + 6, 3, width, plan), silu(pre_first).astype(bf16), jnp.zeros((), bf16)
    )

    ghosts = sides_of(to_here(silu(edge_first).astype(bf16), plan))
    padded_hidden = with_ghosts(hidden_first, ghosts, 3, plan)
    pre_second = convolve(padded_hidden, conv_second)
    hidden_second = silu(pre_second[:, 2:-2]).astype(bf16)
    output = strided_shrink(hidden_second, reduce_kernel_weight).astype(bf16)
    grad_second = (
        upsample_back(wide_cotangent, reduce_kernel_weight) * silu_slope(pre_second)
    ).astype(bf16)

    spread = convolve_back(grad_second, conv_second)
    narrow = spread.astype(bf16)
    theirs, own, corner = exchange(
        narrow[:, :2, 1:-1],
        narrow[:, :-3:-1, 1:-1],
        narrow[:, 1:-1, :2].swapaxes(1, 2),
        narrow[:, 1:-1, :-3:-1].swapaxes(1, 2),
        plan,
    )
    routed = sides_of(to_here(theirs[:, 0], plan))
    grad_first_hidden = add_borders(spread[:, :, 1:-1], routed, 1, plan)
    grad_first = jnp.where(
        inside(strip + 2, 1, width, plan),
        (grad_first_hidden * silu_slope(pre_first[:, 2:-2])).astype(bf16),
        jnp.zeros((), bf16),
    )

    place = jnp.arange(width)[None, :, None]
    corner = corner.astype(f32)
    edge_hidden = (
        theirs[:, 1].astype(f32)
        + to_neighbour(own, plan).astype(f32)
        + jnp.where(place == 0, corner[:, 0, :1], 0.0)
        + jnp.where(place == width - 1, corner[:, 1, :1], 0.0)
    )
    edge_grad = (edge_hidden * silu_slope(edge_first)).astype(bf16)
    routed = sides_of(to_here(neighbour_border(edge_grad, first_kernel_weight, plan), plan))
    spread = convolve_back(grad_first, first_kernel_weight)
    grad_activations = add_borders(spread[:, :, 1:-1], routed, 0, plan).astype(bf16)

    summed = sum_everywhere(
        weight_grad(padded_input[:, 3:-3], grad_first[:, 1:-1])
        + weight_grad(padded_hidden[:, 2:-2], grad_second[:, 2:-2])
        + down_grad(hidden_second, cotangent),
        factor,
    )
    square = (channels, channels)
    return (
        output,
        grad_activations,
        summed[:9].reshape((3, 3) + square),
        summed[9:18].reshape((3, 3) + square),
        summed[18:].reshape((2, 2) + square),
    )


def solution(mesh):
    fine = Mesh(mesh.devices.reshape(XH, Z, CORE, Y, XL), TILE_AXES + ROW_AXES)
    placed = P(TILE_AXES, ROW_AXES, None, None)
    return jax.shard_map(
        body,
        mesh=fine,
        in_specs=(placed, P(), P(), P(), P(), placed),
        out_specs=(placed, placed, P(), P(), P()),
        check_vma=False,
    )
```

```python
import math

import jax
import jax.numpy as jnp
from jax import lax
from jax.sharding import Mesh, PartitionSpec as P

XH, Z, CORE, Y, XL = 2, 8, 2, 4, 2
ROWS = Y * XL
UNITS = 2
TILE_AXES = ("xh", "z", "c")
ROW_AXES = ("y", "xl")
COLUMN_AXES = ("xh", "c")
f32 = jnp.float32
bf16 = jnp.bfloat16


def broadcast_all(piece, axes, count):
    return lax.all_to_all(
        jnp.broadcast_to(piece[None], (count,) + piece.shape), axes, 0, 0, tiled=True
    )


def column_of(group):
    return (group // (Z * CORE)) * CORE + group % CORE


def routing(matching, strip):
    tiles = matching.shape[0]
    here = tiles // (XH * Z * CORE)
    lines = here * 4
    xh, z, core = lax.axis_index("xh"), lax.axis_index("z"), lax.axis_index("c")
    me = xh * CORE + core
    sides = matching.reshape(tiles * 4, 4)
    grouped = matching.reshape(XH, Z, CORE, lines, 4)
    column = lax.dynamic_index_in_dim(grouped, z, 1, keepdims=False).reshape(XH * CORE * lines, 4)
    tile, side = column[:, 0], column[:, 1]
    beside = jnp.where(side < 2, 2, 0)[:, None] + jnp.arange(2)[None, :]
    corners = sides[tile[:, None] * 4 + beside]
    finish = (side[:, None] % 2) ^ corners[..., 2]

    row = lax.axis_index(ROW_AXES)
    cells = UNITS * strip
    piece = cells * lines
    width = ROWS * strip

    def place(tile, side):
        group = tile // here
        held = column_of(group) == me
        return held, ((group // CORE) % Z) * piece + (tile % here) * 4 + side

    def own(table):
        return lax.dynamic_slice_in_dim(table, me * lines, lines, 0)

    held, at = place(tile, side)
    cell = jnp.arange(cells)[None, :, None] * lines
    pick = jnp.where(held.reshape(-1, 1, lines), at.reshape(-1, 1, lines) + cell, -1)
    held, at = place(corners[..., 0], corners[..., 1])
    depth = jnp.arange(2)
    depth = jnp.where(row == 0, depth, strip - 1 - depth)[None, None, :, None] * lines
    held = held.reshape(-1, lines, 2).swapaxes(1, 2)[:, :, None]
    at = at.reshape(-1, lines, 2).swapaxes(1, 2)[:, :, None]
    pick_corner = jnp.where(held, at + depth, -1)
    columns = XH * CORE
    pick = jnp.concatenate(
        [pick.reshape(columns, piece), pick_corner.reshape(columns, 4 * lines)], axis=1
    ).reshape(-1)

    mine, my_corners = own(column), own(corners)
    sent = piece + 4 * lines
    source = column_of(mine[:, 0] // here)[None, :]
    source_corner = column_of(my_corners[..., 0] // here).T[:, None]
    select = jnp.concatenate(
        [
            jnp.broadcast_to(source, (cells, lines)).reshape(-1),
            jnp.broadcast_to(source_corner, (2, 2, lines)).reshape(-1),
        ]
    ) * sent + jnp.arange(sent)

    flip = mine[:, 2:3] == 1
    position = jnp.arange(width)[None, :]
    turned = jnp.where(flip, width - 1 - position, position)
    line = jnp.arange(lines)[:, None]
    return {
        "pick": rows_of(pick, Z * piece),
        "select": rows_of(select, columns * sent),
        "lines": rows_of((position * lines + line).reshape(-1), lines * width),
        "turned": rows_of((turned * lines + line).reshape(-1), lines * width),
        "flip": rows_of((turned + line * width).reshape(-1), lines * width),
        "side": mine[:, 1],
        "quarter": mine[:, 3],
        "quarter_corner": my_corners[..., 3].T,
        "finish": own(finish).T == 1,
        "row": row,
    }


def rows_of(index, count):
    return (index[:, None] == jnp.arange(count)[None, :]).astype(bf16)


def take_rows(choice, rows):
    return jnp.dot(choice, rows, preferred_element_type=f32).astype(bf16)


def turn_channels(lines, quarter):
    half = lines.shape[-1] // 2
    first, second = lines[..., :half], lines[..., half:]
    quarter = quarter.reshape(quarter.shape + (1,) * (lines.ndim - quarter.ndim))
    odd = quarter % 2 == 1
    lead = jnp.where(odd, second, first)
    trail = jnp.where(odd, first, second)
    lead = jnp.where((quarter == 1) | (quarter == 2), -lead, lead)
    trail = jnp.where((quarter == 2) | (quarter == 3), -trail, trail)
    return jnp.concatenate([lead, trail], axis=-1)


def to_here(lines, plan, order="flip"):
    sides = plan["quarter"].shape[0]
    rows = take_rows(plan[order], lines.reshape(-1, lines.shape[-1]))
    return turn_channels(rows.reshape(sides, -1, lines.shape[-1]), plan["quarter"])


def to_neighbour(lines, plan, order="flip"):
    sides = plan["quarter"].shape[0]
    rows = take_rows(plan[order], lines.reshape(-1, lines.shape[-1]))
    return turn_channels(rows.reshape(sides, -1, lines.shape[-1]), (4 - plan["quarter"]) % 4)


def exchange(top, bottom, left, right, plan, later=()):
    units, tiles, width, channels = top.shape
    strip = width // ROWS
    lines = tiles * 4
    line = strip * lines
    piece = units * line
    ends = jnp.where(plan["row"] == ROWS - 1, bottom, top)
    ends = ends.reshape(units, tiles, ROWS, strip, channels).transpose(2, 0, 3, 1, 4)
    ends = lax.all_to_all(
        ends.reshape(ROWS, units * strip * tiles, channels), ROW_AXES, 0, 0, tiled=True
    )
    ends, later = lax.optimization_barrier((ends, later))
    ends = ends.reshape(ROWS, units, strip, tiles, channels)
    pieces = jnp.stack(
        [ends[0], ends[ROWS - 1], left.swapaxes(1, 2), right.swapaxes(1, 2)], axis=3
    ).reshape(piece, channels)
    gathered = broadcast_all(pieces, "z", Z).reshape(Z * piece, channels)
    sent = take_rows(plan["pick"], gathered).reshape(XH * CORE, -1, channels)
    arrived = lax.all_to_all(sent, COLUMN_AXES, 0, 0, tiled=True).reshape(-1, channels)
    mine = jnp.concatenate([take_rows(plan["select"], arrived), pieces[:line]], axis=0)
    whole = broadcast_all(mine, ROW_AXES, ROWS)
    first = whole[:, :line].reshape(ROWS * line, channels)
    second = whole[:, line : 2 * line].reshape(ROWS * line, channels)
    own = whole[:, piece + 4 * lines :].reshape(ROWS * line, channels)
    corner = whole[:, piece : piece + 4 * lines].reshape(ROWS, 2, 2, lines, channels)
    corner = jnp.where(plan["finish"][:, None, :, None], corner[ROWS - 1], corner[0])
    corner = turn_channels(corner, plan["quarter_corner"][:, None])
    return (
        to_here(first, plan, "turned"),
        take_rows(plan["lines"], first).reshape(lines, width, channels),
        take_rows(plan["lines"], second).reshape(lines, width, channels),
        to_neighbour(own, plan, "turned"),
        corner,
        later,
    )


def by_side(cells, plan):
    blocks = [
        jnp.where((plan["side"] == side)[:, None, None], cells, jnp.zeros((), cells.dtype))
        for side in range(4)
    ]
    return jnp.concatenate(blocks, axis=-1)


def neighbour_edge(edge, inner, own, corner, kernel_weight, plan):
    width = own.shape[1]
    w = kernel_weight
    patch = [
        jnp.pad(own, ((0, 0), (1, 1), (0, 0))),
        jnp.concatenate([corner[0, 0][:, None], edge, corner[1, 0][:, None]], axis=1),
        jnp.concatenate([corner[0, 1][:, None], inner, corner[1, 1][:, None]], axis=1),
    ]
    total = None
    for depth in range(3):
        spread = by_side(patch[depth], plan)
        for tap in range(3):
            weights = jnp.concatenate(
                [w[depth, tap], w[2 - depth, tap], w[tap, depth], w[tap, 2 - depth]], axis=0
            )
            term = jnp.dot(spread[:, tap : tap + width], weights, preferred_element_type=f32)
            total = term if total is None else total + term
    return total


def neighbour_border(grads, kernel_weight, plan):
    width = grads.shape[1]
    w = kernel_weight
    spread = by_side(jnp.pad(grads, ((0, 0), (1, 1), (0, 0))), plan)
    total = None
    for tap in range(3):
        weights = jnp.concatenate(
            [w[0, 2 - tap], w[2, 2 - tap], w[2 - tap, 0], w[2 - tap, 2]], axis=1
        )
        term = lax.dot_general(
            spread[:, tap : tap + width],
            weights,
            (((2,), (1,)), ((), ())),
            preferred_element_type=f32,
        )
        total = term if total is None else total + term
    return total


def own_part(lines, margin, plan):
    strip = lines.shape[1] // ROWS
    padded = jnp.pad(lines, ((0, 0), (margin, margin), (0, 0)))
    return lax.dynamic_slice_in_dim(padded, plan["row"] * strip, strip + 2 * margin, 1)


def with_ghosts(strips, ghosts, margin, plan):
    row = plan["row"]
    above = jnp.where(row == 0, ghosts[:, 0], strips[:, margin - 1])
    below = jnp.where(row == ROWS - 1, ghosts[:, 1], strips[:, -margin])
    middle = jnp.concatenate(
        [strips[:, : margin - 1], above[:, None], strips[:, margin:-margin], below[:, None]]
        + ([strips[:, -margin + 1 :]] if margin > 1 else []),
        axis=1,
    )
    left = own_part(ghosts[:, 2], margin, plan)
    right = own_part(ghosts[:, 3], margin, plan)
    return jnp.concatenate([left[:, :, None], middle, right[:, :, None]], axis=2)


def add_borders(interior, routed, margin, plan):
    row = plan["row"]
    routed = routed.astype(f32)
    rows = interior.shape[1]
    index = jnp.arange(rows)[None, :, None, None]
    top = jnp.where((row == 0) & (index == margin), routed[:, 0][:, None], 0.0)
    bottom = jnp.where(
        (row == ROWS - 1) & (index == rows - 1 - margin), routed[:, 1][:, None], 0.0
    )
    column = jnp.arange(interior.shape[2])[None, None, :, None]
    left = own_part(routed[:, 2], margin, plan)[:, :, None]
    right = own_part(routed[:, 3], margin, plan)[:, :, None]
    sides = jnp.where(column == 0, left, 0.0) + jnp.where(
        column == interior.shape[2] - 1, right, 0.0
    )
    return interior + top + bottom + sides


def inside(rows, margin, width, plan):
    strip = width // ROWS
    place = plan["row"] * strip - margin + jnp.arange(rows)
    return ((place >= 0) & (place < width))[None, :, None, None]


def convolve(padded, kernel_weight):
    rows = padded.shape[1] - 2
    columns = padded.shape[2] - 2
    total = None
    for row_tap in range(3):
        for col_tap in range(3):
            term = jnp.dot(
                padded[:, row_tap : row_tap + rows, col_tap : col_tap + columns],
                kernel_weight[row_tap, col_tap],
                preferred_element_type=f32,
            )
            total = term if total is None else total + term
    return total


def convolve_back(grads, kernel_weight):
    rows = grads.shape[1] - 2
    columns = grads.shape[2]
    grads = jnp.pad(grads, ((0, 0), (0, 0), (2, 2), (0, 0)))
    total = None
    for row_tap in range(3):
        for col_tap in range(3):
            term = lax.dot_general(
                grads[:, row_tap : row_tap + rows, col_tap : col_tap + columns + 2],
                kernel_weight[2 - row_tap, 2 - col_tap],
                (((3,), (1,)), ((), ())),
                preferred_element_type=f32,
            )
            total = term if total is None else total + term
    return total


def weight_grad(padded, grads):
    rows = grads.shape[1]
    columns = grads.shape[2]
    return [
        lax.dot_general(
            padded[:, row_tap : row_tap + rows, col_tap : col_tap + columns],
            grads,
            (((0, 1, 2), (0, 1, 2)), ((), ())),
            preferred_element_type=f32,
        )
        for row_tap in range(3)
        for col_tap in range(3)
    ]


def grouped_cells(field):
    tiles, rows, columns, channels = field.shape
    return field.reshape(tiles, rows // 2, 2, columns // 2, 2, channels)


def strided_shrink(field, kernel_weight):
    grouped = grouped_cells(field)
    total = None
    for row_tap in range(2):
        for col_tap in range(2):
            term = jnp.dot(
                grouped[:, :, row_tap, :, col_tap],
                kernel_weight[row_tap, col_tap],
                preferred_element_type=f32,
            )
            total = term if total is None else total + term
    return total


def upsample_back(grads, kernel_weight):
    tiles, rows, columns, channels = grads.shape
    stacked = []
    for row_tap in range(2):
        pieces = [
            lax.dot_general(
                grads,
                kernel_weight[row_tap, col_tap],
                (((3,), (1,)), ((), ())),
                preferred_element_type=f32,
            )
            for col_tap in range(2)
        ]
        stacked.append(jnp.stack(pieces, axis=3))
    return jnp.stack(stacked, axis=2).reshape(tiles, rows * 2, columns * 2, kernel_weight.shape[2])


def down_grad(field, grads):
    grouped = grouped_cells(field)
    return [
        lax.dot_general(
            grouped[:, :, row_tap, :, col_tap],
            grads,
            (((0, 1, 2), (0, 1, 2)), ((), ())),
            preferred_element_type=f32,
        )
        for row_tap in range(2)
        for col_tap in range(2)
    ]


def silu(value):
    return value * jax.nn.sigmoid(value)


def silu_slope(value):
    sigma = jax.nn.sigmoid(value)
    return sigma * (1.0 + value * (1.0 - sigma))


def sum_everywhere(blocks, factor):
    channels = blocks[0].shape[-1]
    count = len(blocks)
    half = count // 2
    core = lax.axis_index("c")
    first = jnp.concatenate(blocks[:half], axis=0)
    second = jnp.concatenate(blocks[half:], axis=0)
    swap = [(0, 1), (1, 0)]
    sent = jnp.where(core == 0, second, first).astype(bf16)
    held = jnp.where(core == 0, first, second) + lax.ppermute(sent, "c", swap).astype(f32)
    held = held.astype(bf16).reshape(ROWS, -1, channels)
    held = lax.all_to_all(held, ROW_AXES, 0, 0, tiled=True).astype(f32).sum(0)
    held = held.astype(bf16).reshape(XH * Z, -1, channels)
    held = lax.all_to_all(held, ("xh", "z"), 0, 0, tiled=True).astype(f32).sum(0)
    held = (held * factor).astype(bf16)
    held = broadcast_all(held, ("xh", "z"), XH * Z).reshape(-1, channels)
    held = broadcast_all(held, ROW_AXES, ROWS).reshape(-1, channels)
    other = lax.ppermute(held, "c", swap)
    first = jnp.where(core == 0, held, other)
    second = jnp.where(core == 0, other, held)
    both = jnp.concatenate([first, second], axis=0).astype(f32)
    return both.reshape(count, channels, channels)


def body(activations, matching, first_kernel_weight, conv_second, reduce_kernel_weight, cotangent):
    tiles, strip, width, channels = activations.shape
    plan = routing(matching, strip)
    factor = 1.0 / math.sqrt(matching.shape[0] * width * width)

    first_rows = jnp.concatenate(
        [activations[:, :4].reshape(tiles, 4 * width, channels), cotangent[:, 0]], axis=1
    )
    last_rows = jnp.concatenate(
        [activations[:, -4:].reshape(tiles, 4 * width, channels), cotangent[:, -1]], axis=1
    )
    def sides_of(lines):
        return lines.reshape(tiles, 4, width, channels)

    ghosts, edge, inner, own, corner, (first_rows, last_rows) = exchange(
        jnp.stack([activations[:, 0], activations[:, 1]]),
        jnp.stack([activations[:, -1], activations[:, -2]]),
        jnp.stack([activations[:, :, 0], activations[:, :, 1]]),
        jnp.stack([activations[:, :, -1], activations[:, :, -2]]),
        plan,
        (first_rows, last_rows),
    )
    above = lax.ppermute(last_rows, ROW_AXES, [(i, i + 1) for i in range(ROWS - 1)])
    below = lax.ppermute(first_rows, ROW_AXES, [(i + 1, i) for i in range(ROWS - 1)])
    cells = 4 * width
    wide_input = jnp.concatenate(
        [
            above[:, :cells].reshape(tiles, 4, width, channels),
            activations,
            below[:, :cells].reshape(tiles, 4, width, channels),
        ],
        axis=1,
    )
    wide_cotangent = jnp.concatenate(
        [above[:, None, cells:], cotangent, below[:, None, cells:]], axis=1
    )

    edge_first = neighbour_edge(edge, inner, own, corner, first_kernel_weight, plan)
    padded_input = with_ghosts(wide_input, sides_of(ghosts), 4, plan)
    pre_first = convolve(padded_input, first_kernel_weight)
    hidden_first = jnp.where(
        inside(strip + 6, 3, width, plan), silu(pre_first).astype(bf16), jnp.zeros((), bf16)
    )

    ghosts = sides_of(to_here(silu(edge_first).astype(bf16), plan))
    padded_hidden = with_ghosts(hidden_first, ghosts, 3, plan)
    pre_second = convolve(padded_hidden, conv_second)
    hidden_second = silu(pre_second[:, 2:-2]).astype(bf16)
    output = strided_shrink(hidden_second, reduce_kernel_weight).astype(bf16)
    grad_second = (
        upsample_back(wide_cotangent, reduce_kernel_weight) * silu_slope(pre_second)
    ).astype(bf16)

    spread = convolve_back(grad_second, conv_second)
    narrow = spread.astype(bf16)
    routed, _, inner, own, corner, _ = exchange(
        jnp.stack([narrow[:, 0, 1:-1], narrow[:, 1, 1:-1]]),
        jnp.stack([narrow[:, -1, 1:-1], narrow[:, -2, 1:-1]]),
        jnp.stack([narrow[:, 1:-1, 0], narrow[:, 1:-1, 1]]),
        jnp.stack([narrow[:, 1:-1, -1], narrow[:, 1:-1, -2]]),
        plan,
    )
    routed = sides_of(routed)
    grad_first_hidden = add_borders(spread[:, :, 1:-1], routed, 1, plan)
    grad_first = jnp.where(
        inside(strip + 2, 1, width, plan),
        (grad_first_hidden * silu_slope(pre_first[:, 2:-2])).astype(bf16),
        jnp.zeros((), bf16),
    )

    place = jnp.arange(width)[None, :, None]
    corner = corner.astype(f32)
    edge_hidden = (
        inner.astype(f32)
        + own.astype(f32)
        + jnp.where(place == 0, corner[0, 0][:, None], 0.0)
        + jnp.where(place == width - 1, corner[1, 0][:, None], 0.0)
    )
    edge_grad = (edge_hidden * silu_slope(edge_first)).astype(bf16)
    routed = sides_of(to_here(neighbour_border(edge_grad, first_kernel_weight, plan).astype(bf16), plan))
    spread = convolve_back(grad_first, first_kernel_weight)
    grad_activations = add_borders(spread[:, :, 1:-1], routed, 0, plan).astype(bf16)

    summed = sum_everywhere(
        weight_grad(padded_input[:, 3:-3], grad_first[:, 1:-1])
        + weight_grad(padded_hidden[:, 2:-2], grad_second[:, 2:-2])
        + down_grad(hidden_second, cotangent),
        factor,
    )
    square = (channels, channels)
    return (
        output,
        grad_activations,
        summed[:9].reshape((3, 3) + square),
        summed[9:18].reshape((3, 3) + square),
        summed[18:].reshape((2, 2) + square),
    )


def solution(mesh):
    fine = Mesh(mesh.devices.reshape(XH, Z, CORE, Y, XL), TILE_AXES + ROW_AXES)
    placed = P(TILE_AXES, ROW_AXES, None, None)
    return jax.shard_map(
        body,
        mesh=fine,
        in_specs=(placed, P(), P(), P(), P(), placed),
        out_specs=(placed, placed, P(), P(), P()),
        check_vma=False,
    )
```

```python
import math

import jax
import jax.numpy as jnp
from jax import lax
from jax.sharding import Mesh, PartitionSpec as P

XH, Z, CORE, Y, XL = 2, 8, 2, 4, 2
ROWS = Y * XL
UNITS = 2
EXTRA = 6
TILE_AXES = ("xh", "z", "c")
ROW_AXES = ("y", "xl")
COLUMN_AXES = ("xh", "c")
f32 = jnp.float32
bf16 = jnp.bfloat16


def broadcast_all(piece, axes, count):
    return lax.all_to_all(
        jnp.broadcast_to(piece[None], (count,) + piece.shape), axes, 0, 0, tiled=True
    )


def column_of(group):
    return (group // (Z * CORE)) * CORE + group % CORE


def routing(matching, strip):
    tiles = matching.shape[0]
    here = tiles // (XH * Z * CORE)
    lines = here * 4
    xh, z, core = lax.axis_index("xh"), lax.axis_index("z"), lax.axis_index("c")
    me = xh * CORE + core
    sides = matching.reshape(tiles * 4, 4)
    grouped = matching.reshape(XH, Z, CORE, lines, 4)
    column = lax.dynamic_index_in_dim(grouped, z, 1, keepdims=False).reshape(XH * CORE * lines, 4)
    tile, side = column[:, 0], column[:, 1]
    beside = jnp.where(side < 2, 2, 0)[:, None] + jnp.arange(2)[None, :]
    corners = sides[tile[:, None] * 4 + beside]
    finish = (side[:, None] % 2) ^ corners[..., 2]

    row = lax.axis_index(ROW_AXES)
    cells = UNITS * strip
    piece = cells * lines
    width = ROWS * strip

    def place(tile, side):
        group = tile // here
        held = column_of(group) == me
        return held, ((group // CORE) % Z) * piece + (tile % here) * 4 + side

    def own(table):
        return lax.dynamic_slice_in_dim(table, me * lines, lines, 0)

    held, at = place(tile, side)
    cell = jnp.arange(cells)[None, :, None] * lines
    pick = jnp.where(held.reshape(-1, 1, lines), at.reshape(-1, 1, lines) + cell, -1)
    held, at = place(corners[..., 0], corners[..., 1])
    depth = jnp.arange(2)
    depth = jnp.where(row == 0, depth, strip - 1 - depth)[None, None, :, None] * lines
    held = held.reshape(-1, lines, 2).swapaxes(1, 2)[:, :, None]
    at = at.reshape(-1, lines, 2).swapaxes(1, 2)[:, :, None]
    pick_corner = jnp.where(held, at + depth, -1)
    columns = XH * CORE
    pick = jnp.concatenate(
        [pick.reshape(columns, piece), pick_corner.reshape(columns, 4 * lines)], axis=1
    ).reshape(-1)

    mine, my_corners = own(column), own(corners)
    sent = piece + 4 * lines
    source = column_of(mine[:, 0] // here)[None, :]
    source_corner = column_of(my_corners[..., 0] // here).T[:, None]
    select = jnp.concatenate(
        [
            jnp.broadcast_to(source, (cells, lines)).reshape(-1),
            jnp.broadcast_to(source_corner, (2, 2, lines)).reshape(-1),
        ]
    ) * sent + jnp.arange(sent)

    flip = mine[:, 2:3] == 1
    position = jnp.arange(width)[None, :]
    turned = jnp.where(flip, width - 1 - position, position)
    line = jnp.arange(lines)[:, None]
    return {
        "pick": rows_of(pick, Z * piece),
        "select": rows_of(select, columns * sent),
        "lines": rows_of((position * lines + line).reshape(-1), lines * width),
        "turned": rows_of((turned * lines + line).reshape(-1), lines * width),
        "flip": rows_of((turned + line * width).reshape(-1), lines * width),
        "turned_at": turned,
        "side": mine[:, 1],
        "quarter": mine[:, 3],
        "quarter_corner": my_corners[..., 3].T,
        "finish": own(finish).T == 1,
        "row": row,
    }


def rows_of(index, count):
    return (index[:, None] == jnp.arange(count)[None, :]).astype(bf16)


def take_rows(choice, rows):
    return jnp.dot(choice, rows, preferred_element_type=f32).astype(bf16)


def turn_channels(lines, quarter):
    half = lines.shape[-1] // 2
    first, second = lines[..., :half], lines[..., half:]
    quarter = quarter.reshape(quarter.shape + (1,) * (lines.ndim - quarter.ndim))
    odd = quarter % 2 == 1
    lead = jnp.where(odd, second, first)
    trail = jnp.where(odd, first, second)
    lead = jnp.where((quarter == 1) | (quarter == 2), -lead, lead)
    trail = jnp.where((quarter == 2) | (quarter == 3), -trail, trail)
    return jnp.concatenate([lead, trail], axis=-1)


def to_here(lines, plan, order="flip"):
    sides = plan["quarter"].shape[0]
    rows = take_rows(plan[order], lines.reshape(-1, lines.shape[-1]))
    return turn_channels(rows.reshape(sides, -1, lines.shape[-1]), plan["quarter"])


def to_neighbour(lines, plan, order="flip"):
    sides = plan["quarter"].shape[0]
    rows = take_rows(plan[order], lines.reshape(-1, lines.shape[-1]))
    return turn_channels(rows.reshape(sides, -1, lines.shape[-1]), (4 - plan["quarter"]) % 4)


def outer_lines(field, margin, row):
    tiles, rows, columns, channels = field.shape
    strip = rows - 2 * margin
    width = ROWS * strip
    unit = jnp.arange(UNITS)[:, None, None]
    cell = jnp.arange(strip)[None, :, None]
    tile = jnp.arange(tiles)[None, None, :] * (rows * columns)
    line = jnp.where(row == ROWS - 1, rows - 1 - unit, unit)
    target = jnp.arange(ROWS)[:, None, None, None]
    ends = tile + line * columns + margin + target * strip + cell
    last = width + 2 * margin - 1
    sides = jnp.stack([unit + tile, last - unit + tile], axis=-1) + (margin + cell)[..., None] * columns
    index = jnp.concatenate([ends.reshape(-1), sides.reshape(-1)])
    chosen = take_rows(rows_of(index, tiles * rows * columns), field.reshape(-1, channels))
    cut = ROWS * UNITS * strip * tiles
    return chosen[:cut].reshape(ROWS, -1, channels), chosen[cut:]


def own_borders(field, plan):
    tiles, rows, columns, channels = field.shape
    strip = rows - 2
    width = ROWS * strip
    row = plan["row"]
    at = plan["turned_at"].reshape(tiles, 4, width)
    side = jnp.arange(4)[None, :, None]
    tile = jnp.arange(tiles)[:, None, None] * (rows * columns)
    end = jnp.where(side == 0, 1 + at, (rows - 1) * columns + 1 + at)
    along = (1 + at - row * strip) * columns + jnp.where(side == 2, 0, width + 1)
    index = tile + jnp.where(side < 2, end, along)
    mine = jnp.where(side < 2, row == side * (ROWS - 1), at // strip == row)
    index = jnp.where(mine, index, -1).reshape(-1)
    chosen = take_rows(rows_of(index, tiles * rows * columns), field.reshape(-1, channels))
    return turn_channels(chosen.reshape(tiles * 4, width, channels), (4 - plan["quarter"]) % 4)


def share_ends(ends):
    return lax.all_to_all(ends, ROW_AXES, 0, 0, tiled=True)


def exchange(ends, sides, tiles, plan, rider=None):
    channels = sides.shape[-1]
    lines = tiles * 4
    strip = sides.shape[0] // (UNITS * tiles * 2)
    width = ROWS * strip
    line = strip * lines
    piece = UNITS * line
    held = jnp.concatenate([ends[0], ends[ROWS - 1], sides], axis=0)
    order = jnp.arange(UNITS * strip * tiles)[:, None]
    half = UNITS * strip * tiles
    order = jnp.concatenate(
        [order, half + order, 2 * half + 2 * order, 2 * half + 2 * order + 1], axis=1
    ).reshape(-1)
    everywhere = jnp.broadcast_to(order, (Z, piece)).reshape(-1)
    spread = take_rows(rows_of(everywhere, piece), held).reshape(Z, piece, channels)
    gathered = lax.all_to_all(spread, "z", 0, 0, tiled=True).reshape(Z * piece, channels)
    sent = take_rows(plan["pick"], gathered).reshape(XH * CORE, -1, channels)
    arrived = lax.all_to_all(sent, COLUMN_AXES, 0, 0, tiled=True).reshape(-1, channels)
    first_own = take_rows(rows_of(order[:line], piece), held)
    mine = jnp.concatenate([take_rows(plan["select"], arrived), first_own], axis=0)
    count = mine.shape[0]
    mine = jnp.broadcast_to(mine[None], (ROWS,) + mine.shape)
    if rider is not None:
        mine = jnp.concatenate([mine, rider], axis=1)
    whole = lax.all_to_all(mine, ROW_AXES, 0, 0, tiled=True)
    first = whole[:, :line].reshape(ROWS * line, channels)
    second = whole[:, line : 2 * line].reshape(ROWS * line, channels)
    own = whole[:, piece + 4 * lines : count].reshape(ROWS * line, channels)
    corner = whole[:, piece : piece + 4 * lines].reshape(ROWS, 2, 2, lines, channels)
    corner = jnp.where(plan["finish"][:, None, :, None], corner[ROWS - 1], corner[0])
    corner = turn_channels(corner, plan["quarter_corner"][:, None])
    return (
        to_here(first, plan, "turned"),
        take_rows(plan["lines"], first).reshape(lines, width, channels),
        take_rows(plan["lines"], second).reshape(lines, width, channels),
        to_neighbour(own, plan, "turned"),
        corner,
        whole[:, count:],
    )


def by_side(cells, plan):
    blocks = [
        jnp.where((plan["side"] == side)[:, None, None], cells, jnp.zeros((), cells.dtype))
        for side in range(4)
    ]
    return jnp.concatenate(blocks, axis=-1)


def neighbour_edge(edge, inner, own, corner, kernel_weight, plan):
    width = own.shape[1]
    w = kernel_weight
    patch = [
        jnp.pad(own, ((0, 0), (1, 1), (0, 0))),
        jnp.concatenate([corner[0, 0][:, None], edge, corner[1, 0][:, None]], axis=1),
        jnp.concatenate([corner[0, 1][:, None], inner, corner[1, 1][:, None]], axis=1),
    ]
    total = None
    spreads = [by_side(cells, plan) for cells in patch]
    for depth in range(3):
        spread = spreads[depth]
        for tap in range(3):
            weights = jnp.concatenate(
                [w[depth, tap], w[2 - depth, tap], w[tap, depth], w[tap, 2 - depth]], axis=0
            )
            term = jnp.dot(spread[:, tap : tap + width], weights, preferred_element_type=f32)
            total = term if total is None else total + term
    return total, spreads


def neighbour_weight_grad(spreads, grads):
    width = grads.shape[1]
    channels = grads.shape[2]
    terms = [
        [
            lax.dot_general(
                spreads[depth][:, tap : tap + width],
                grads,
                (((0, 1), (0, 1)), ((), ())),
                preferred_element_type=f32,
            ).reshape(4, channels, channels)
            for tap in range(3)
        ]
        for depth in range(3)
    ]
    return [
        terms[a][b][0] + terms[2 - a][b][1] + terms[b][a][2] + terms[2 - b][a][3]
        for a in range(3)
        for b in range(3)
    ]


def neighbour_border(grads, kernel_weight, plan):
    width = grads.shape[1]
    w = kernel_weight
    spread = by_side(jnp.pad(grads, ((0, 0), (1, 1), (0, 0))), plan)
    total = None
    for tap in range(3):
        weights = jnp.concatenate(
            [w[0, 2 - tap], w[2, 2 - tap], w[2 - tap, 0], w[2 - tap, 2]], axis=1
        )
        term = lax.dot_general(
            spread[:, tap : tap + width],
            weights,
            (((2,), (1,)), ((), ())),
            preferred_element_type=f32,
        )
        total = term if total is None else total + term
    return total


def own_part(lines, margin, plan):
    strip = lines.shape[1] // ROWS
    padded = jnp.pad(lines, ((0, 0), (margin, margin), (0, 0)))
    return lax.dynamic_slice_in_dim(padded, plan["row"] * strip, strip + 2 * margin, 1)


def with_ghosts(strips, ghosts, margin, plan):
    row = plan["row"]
    above = jnp.where(row == 0, ghosts[:, 0], strips[:, margin - 1])
    below = jnp.where(row == ROWS - 1, ghosts[:, 1], strips[:, -margin])
    middle = jnp.concatenate(
        [strips[:, : margin - 1], above[:, None], strips[:, margin:-margin], below[:, None]]
        + ([strips[:, -margin + 1 :]] if margin > 1 else []),
        axis=1,
    )
    left = own_part(ghosts[:, 2], margin, plan)
    right = own_part(ghosts[:, 3], margin, plan)
    return jnp.concatenate([left[:, :, None], middle, right[:, :, None]], axis=2)


def add_borders(interior, routed, margin, plan):
    row = plan["row"]
    routed = routed.astype(f32)
    rows = interior.shape[1]
    index = jnp.arange(rows)[None, :, None, None]
    top = jnp.where((row == 0) & (index == margin), routed[:, 0][:, None], 0.0)
    bottom = jnp.where(
        (row == ROWS - 1) & (index == rows - 1 - margin), routed[:, 1][:, None], 0.0
    )
    column = jnp.arange(interior.shape[2])[None, None, :, None]
    left = own_part(routed[:, 2], margin, plan)[:, :, None]
    right = own_part(routed[:, 3], margin, plan)[:, :, None]
    sides = jnp.where(column == 0, left, 0.0) + jnp.where(
        column == interior.shape[2] - 1, right, 0.0
    )
    return interior + top + bottom + sides


def inside(rows, margin, width, plan):
    strip = width // ROWS
    place = plan["row"] * strip - margin + jnp.arange(rows)
    return ((place >= 0) & (place < width))[None, :, None, None]


def convolve(padded, kernel_weight):
    rows = padded.shape[1] - 2
    columns = padded.shape[2] - 2
    total = None
    for row_tap in range(3):
        for col_tap in range(3):
            term = jnp.dot(
                padded[:, row_tap : row_tap + rows, col_tap : col_tap + columns],
                kernel_weight[row_tap, col_tap],
                preferred_element_type=f32,
            )
            total = term if total is None else total + term
    return total


def convolve_back(grads, kernel_weight, extra=0):
    rows = grads.shape[1] - 2
    columns = grads.shape[2] + extra
    grads = jnp.pad(grads, ((0, 0), (0, 0), (2, 2 + extra), (0, 0)))
    total = None
    for row_tap in range(3):
        for col_tap in range(3):
            term = lax.dot_general(
                grads[:, row_tap : row_tap + rows, col_tap : col_tap + columns + 2],
                kernel_weight[2 - row_tap, 2 - col_tap],
                (((3,), (1,)), ((), ())),
                preferred_element_type=f32,
            )
            total = term if total is None else total + term
    return total


def weight_grad(padded, grads):
    rows = grads.shape[1]
    columns = grads.shape[2]
    return [
        lax.dot_general(
            padded[:, row_tap : row_tap + rows, col_tap : col_tap + columns],
            grads,
            (((0, 1, 2), (0, 1, 2)), ((), ())),
            preferred_element_type=f32,
        )
        for row_tap in range(3)
        for col_tap in range(3)
    ]


def grouped_cells(field):
    tiles, rows, columns, channels = field.shape
    return field.reshape(tiles, rows // 2, 2, columns // 2, 2, channels)


def strided_shrink(field, kernel_weight):
    grouped = grouped_cells(field)
    total = None
    for row_tap in range(2):
        for col_tap in range(2):
            term = jnp.dot(
                grouped[:, :, row_tap, :, col_tap],
                kernel_weight[row_tap, col_tap],
                preferred_element_type=f32,
            )
            total = term if total is None else total + term
    return total


def upsample_back(grads, kernel_weight):
    tiles, rows, columns, channels = grads.shape
    stacked = []
    for row_tap in range(2):
        pieces = [
            lax.dot_general(
                grads,
                kernel_weight[row_tap, col_tap],
                (((3,), (1,)), ((), ())),
                preferred_element_type=f32,
            )
            for col_tap in range(2)
        ]
        stacked.append(jnp.stack(pieces, axis=3))
    return jnp.stack(stacked, axis=2).reshape(tiles, rows * 2, columns * 2, kernel_weight.shape[2])


def down_grad(field, grads):
    grouped = grouped_cells(field)
    return [
        lax.dot_general(
            grouped[:, :, row_tap, :, col_tap],
            grads,
            (((0, 1, 2), (0, 1, 2)), ((), ())),
            preferred_element_type=f32,
        )
        for row_tap in range(2)
        for col_tap in range(2)
    ]


def silu(value):
    return value * jax.nn.sigmoid(value)


def silu_slope(value):
    sigma = jax.nn.sigmoid(value)
    return sigma * (1.0 + value * (1.0 - sigma))


SWAP = [(0, 1), (1, 0)]


def sum_pair(blocks):
    channels = blocks[0].shape[-1]
    half = len(blocks) // 2
    core = lax.axis_index("c")
    first = jnp.concatenate(blocks[:half], axis=0)
    second = jnp.concatenate(blocks[half:], axis=0)
    sent = jnp.where(core == 0, second, first).astype(bf16)
    held = jnp.where(core == 0, first, second) + lax.ppermute(sent, "c", SWAP).astype(f32)
    return held.astype(bf16).reshape(ROWS, -1, channels)


def sum_rest(held, factor):
    channels = held.shape[-1]
    core = lax.axis_index("c")
    held = held.astype(f32).sum(0)
    held = held.astype(bf16).reshape(XH * Z, -1, channels)
    held = lax.all_to_all(held, ("xh", "z"), 0, 0, tiled=True).astype(f32).sum(0)
    held = (held * factor).astype(bf16)
    held = broadcast_all(held, ("xh", "z"), XH * Z).reshape(-1, channels)
    held = broadcast_all(held, ROW_AXES, ROWS).reshape(-1, channels)
    other = lax.ppermute(held, "c", SWAP)
    first = jnp.where(core == 0, held, other)
    second = jnp.where(core == 0, other, held)
    return jnp.concatenate([first, second], axis=0).astype(f32).reshape(-1, channels, channels)


def body(activations, matching, first_kernel_weight, conv_second, reduce_kernel_weight, cotangent):
    tiles, strip, width, channels = activations.shape
    factor = 1.0 / math.sqrt(matching.shape[0] * width * width)

    first_rows = jnp.concatenate(
        [activations[:, :4].reshape(tiles, 4 * width, channels), cotangent[:, 0]], axis=1
    )
    last_rows = jnp.concatenate(
        [activations[:, -4:].reshape(tiles, 4 * width, channels), cotangent[:, -1]], axis=1
    )
    def sides_of(lines):
        return lines.reshape(tiles, 4, width, channels)

    ends, sides = outer_lines(activations, 0, lax.axis_index(ROW_AXES))
    ends = share_ends(ends)
    ends, first_rows, last_rows, matching = lax.optimization_barrier(
        (ends, first_rows, last_rows, matching)
    )
    plan = routing(matching, strip)
    ghosts, edge, inner, own, corner, _ = exchange(ends, sides, tiles, plan)
    above = lax.ppermute(last_rows, ROW_AXES, [(i, i + 1) for i in range(ROWS - 1)])
    below = lax.ppermute(first_rows, ROW_AXES, [(i + 1, i) for i in range(ROWS - 1)])
    cells = 4 * width
    wide_input = jnp.concatenate(
        [
            above[:, :cells].reshape(tiles, 4, width, channels),
            activations,
            below[:, :cells].reshape(tiles, 4, width, channels),
        ],
        axis=1,
    )
    wide_cotangent = jnp.concatenate(
        [above[:, None, cells:], cotangent, below[:, None, cells:]], axis=1
    )

    edge_first, edge_cells = neighbour_edge(edge, inner, own, corner, first_kernel_weight, plan)
    padded_input = with_ghosts(wide_input, sides_of(ghosts), 4, plan)
    pre_first = convolve(padded_input, first_kernel_weight)
    hidden_first = jnp.where(
        inside(strip + 6, 3, width, plan), silu(pre_first).astype(bf16), jnp.zeros((), bf16)
    )

    ghosts = sides_of(to_here(silu(edge_first).astype(bf16), plan))
    padded_hidden = with_ghosts(hidden_first, ghosts, 3, plan)
    pre_second = convolve(padded_hidden, conv_second)
    hidden_second = silu(pre_second[:, 2:-2]).astype(bf16)
    output = strided_shrink(hidden_second, reduce_kernel_weight).astype(bf16)
    grad_second = (
        upsample_back(wide_cotangent, reduce_kernel_weight) * silu_slope(pre_second)
    ).astype(bf16)

    spread = convolve_back(grad_second, conv_second, EXTRA)
    narrow = spread.astype(bf16)
    ends, sides = outer_lines(narrow, 1, plan["row"])
    ends = share_ends(ends)

    edge_slope = silu_slope(edge_first)
    slope_first = silu_slope(pre_first[:, 2:-2])
    own_grad = (spread[:, 1:-1, 1 : width + 1] * slope_first[:, 1:-1]).astype(bf16)
    border_grad = (own_borders(narrow, plan).astype(f32) * edge_slope).astype(bf16)
    own_terms = weight_grad(padded_input[:, 3:-3], own_grad)
    border_terms = neighbour_weight_grad(edge_cells, border_grad)
    parts = sum_pair(
        [one + two for one, two in zip(own_terms, border_terms)]
        + weight_grad(padded_hidden[:, 2:-2], grad_second[:, 2:-2])
        + down_grad(hidden_second, cotangent)
    )

    routed, _, inner, own, corner, parts = exchange(ends, sides, tiles, plan, parts)
    routed = sides_of(routed)
    grad_first_hidden = add_borders(spread[:, :, 1 : width + 1], routed, 1, plan)
    grad_first = jnp.where(
        inside(strip + 2, 1, width, plan),
        (grad_first_hidden * slope_first).astype(bf16),
        jnp.zeros((), bf16),
    )

    place = jnp.arange(width)[None, :, None]
    corner = corner.astype(f32)
    edge_hidden = (
        inner.astype(f32)
        + own.astype(f32)
        + jnp.where(place == 0, corner[0, 0][:, None], 0.0)
        + jnp.where(place == width - 1, corner[1, 0][:, None], 0.0)
    )
    edge_grad = (edge_hidden * edge_slope).astype(bf16)
    routed = sides_of(to_here(neighbour_border(edge_grad, first_kernel_weight, plan).astype(bf16), plan))
    spread = convolve_back(grad_first, first_kernel_weight)
    grad_activations = add_borders(spread[:, :, 1:-1], routed, 0, plan).astype(bf16)

    summed = sum_rest(parts, factor)
    square = (channels, channels)
    return (
        output,
        grad_activations,
        summed[:9].reshape((3, 3) + square),
        summed[9:18].reshape((3, 3) + square),
        summed[18:].reshape((2, 2) + square),
    )


def solution(mesh):
    fine = Mesh(mesh.devices.reshape(XH, Z, CORE, Y, XL), TILE_AXES + ROW_AXES)
    placed = P(TILE_AXES, ROW_AXES, None, None)
    return jax.shard_map(
        body,
        mesh=fine,
        in_specs=(placed, P(), P(), P(), P(), placed),
        out_specs=(placed, placed, P(), P(), P()),
        check_vma=False,
    )
```

```python
import math

import jax
import jax.numpy as jnp
from jax import lax
from jax.experimental import pallas as pl
from jax.experimental.pallas import tpu as pltpu
from jax.sharding import Mesh, PartitionSpec as P

XH, Z, CORE, Y, XL = 2, 8, 2, 4, 2
ROWS = Y * XL
UNITS = 2
EXTRA = 6
TILE_AXES = ("xh", "z", "c")
ROW_AXES = ("y", "xl")
COLUMN_AXES = ("xh", "c")
f32 = jnp.float32
bf16 = jnp.bfloat16


def broadcast_all(piece, axes, count):
    return lax.all_to_all(
        jnp.broadcast_to(piece[None], (count,) + piece.shape), axes, 0, 0, tiled=True
    )


def column_of(group):
    return (group // (Z * CORE)) * CORE + group % CORE


def routing(matching, strip):
    tiles = matching.shape[0]
    here = tiles // (XH * Z * CORE)
    lines = here * 4
    xh, z, core = lax.axis_index("xh"), lax.axis_index("z"), lax.axis_index("c")
    me = xh * CORE + core
    sides = matching.reshape(tiles * 4, 4)
    grouped = matching.reshape(XH, Z, CORE, lines, 4)
    column = lax.dynamic_index_in_dim(grouped, z, 1, keepdims=False).reshape(XH * CORE * lines, 4)
    tile, side = column[:, 0], column[:, 1]
    beside = jnp.where(side < 2, 2, 0)[:, None] + jnp.arange(2)[None, :]
    corners = sides[tile[:, None] * 4 + beside]
    finish = (side[:, None] % 2) ^ corners[..., 2]

    row = lax.axis_index(ROW_AXES)
    cells = UNITS * strip
    piece = cells * lines
    width = ROWS * strip

    def place(tile, side):
        group = tile // here
        held = column_of(group) == me
        return held, ((group // CORE) % Z) * piece + (tile % here) * 4 + side

    def own(table):
        return lax.dynamic_slice_in_dim(table, me * lines, lines, 0)

    held, at = place(tile, side)
    cell = jnp.arange(cells)[None, :, None] * lines
    pick = jnp.where(held.reshape(-1, 1, lines), at.reshape(-1, 1, lines) + cell, -1)
    held, at = place(corners[..., 0], corners[..., 1])
    depth = jnp.arange(2)
    depth = jnp.where(row == 0, depth, strip - 1 - depth)[None, None, :, None] * lines
    held = held.reshape(-1, lines, 2).swapaxes(1, 2)[:, :, None]
    at = at.reshape(-1, lines, 2).swapaxes(1, 2)[:, :, None]
    pick_corner = jnp.where(held, at + depth, -1)
    columns = XH * CORE
    pick = jnp.concatenate(
        [pick.reshape(columns, piece), pick_corner.reshape(columns, 4 * lines)], axis=1
    ).reshape(-1)

    mine, my_corners = own(column), own(corners)
    sent = piece + 4 * lines
    source = column_of(mine[:, 0] // here)[None, :]
    source_corner = column_of(my_corners[..., 0] // here).T[:, None]
    select = jnp.concatenate(
        [
            jnp.broadcast_to(source, (cells, lines)).reshape(-1),
            jnp.broadcast_to(source_corner, (2, 2, lines)).reshape(-1),
        ]
    ) * sent + jnp.arange(sent)

    flip = mine[:, 2:3] == 1
    position = jnp.arange(width)[None, :]
    turned = jnp.where(flip, width - 1 - position, position)
    line = jnp.arange(lines)[:, None]
    return {
        "pick": rows_of(pick, Z * piece),
        "select": rows_of(select, columns * sent),
        "lines": rows_of((position * lines + line).reshape(-1), lines * width),
        "turned": rows_of((turned * lines + line).reshape(-1), lines * width),
        "flip": rows_of((turned + line * width).reshape(-1), lines * width),
        "turned_at": turned,
        "side": mine[:, 1],
        "quarter": mine[:, 3],
        "quarter_corner": my_corners[..., 3].T,
        "finish": own(finish).T == 1,
        "row": row,
    }


def rows_of(index, count):
    return (index[:, None] == jnp.arange(count)[None, :]).astype(bf16)


def take_rows(choice, rows):
    return jnp.dot(choice, rows, preferred_element_type=f32).astype(bf16)


def turn_channels(lines, quarter):
    half = lines.shape[-1] // 2
    first, second = lines[..., :half], lines[..., half:]
    quarter = quarter.reshape(quarter.shape + (1,) * (lines.ndim - quarter.ndim))
    odd = quarter % 2 == 1
    lead = jnp.where(odd, second, first)
    trail = jnp.where(odd, first, second)
    lead = jnp.where((quarter == 1) | (quarter == 2), -lead, lead)
    trail = jnp.where((quarter == 2) | (quarter == 3), -trail, trail)
    return jnp.concatenate([lead, trail], axis=-1)


def to_here(lines, plan, order="flip"):
    sides = plan["quarter"].shape[0]
    rows = take_rows(plan[order], lines.reshape(-1, lines.shape[-1]))
    return turn_channels(rows.reshape(sides, -1, lines.shape[-1]), plan["quarter"])


def to_neighbour(lines, plan, order="flip"):
    sides = plan["quarter"].shape[0]
    rows = take_rows(plan[order], lines.reshape(-1, lines.shape[-1]))
    return turn_channels(rows.reshape(sides, -1, lines.shape[-1]), (4 - plan["quarter"]) % 4)


def outer_lines(field, margin, row):
    tiles, rows, columns, channels = field.shape
    strip = rows - 2 * margin
    width = ROWS * strip
    unit = jnp.arange(UNITS)[:, None, None]
    cell = jnp.arange(strip)[None, :, None]
    tile = jnp.arange(tiles)[None, None, :] * (rows * columns)
    line = jnp.where(row == ROWS - 1, rows - 1 - unit, unit)
    target = jnp.arange(ROWS)[:, None, None, None]
    ends = tile + line * columns + margin + target * strip + cell
    last = width + 2 * margin - 1
    sides = jnp.stack([unit + tile, last - unit + tile], axis=-1) + (margin + cell)[..., None] * columns
    index = jnp.concatenate([ends.reshape(-1), sides.reshape(-1)])
    chosen = take_rows(rows_of(index, tiles * rows * columns), field.reshape(-1, channels))
    cut = ROWS * UNITS * strip * tiles
    return chosen[:cut].reshape(ROWS, -1, channels), chosen[cut:]


def own_borders(field, plan):
    tiles, rows, columns, channels = field.shape
    strip = rows - 2
    width = ROWS * strip
    row = plan["row"]
    at = plan["turned_at"].reshape(tiles, 4, width)
    side = jnp.arange(4)[None, :, None]
    tile = jnp.arange(tiles)[:, None, None] * (rows * columns)
    end = jnp.where(side == 0, 1 + at, (rows - 1) * columns + 1 + at)
    along = (1 + at - row * strip) * columns + jnp.where(side == 2, 0, width + 1)
    index = tile + jnp.where(side < 2, end, along)
    mine = jnp.where(side < 2, row == side * (ROWS - 1), at // strip == row)
    index = jnp.where(mine, index, -1).reshape(-1)
    chosen = take_rows(rows_of(index, tiles * rows * columns), field.reshape(-1, channels))
    return turn_channels(chosen.reshape(tiles * 4, width, channels), (4 - plan["quarter"]) % 4)


def share_ends(ends):
    return lax.all_to_all(ends, ROW_AXES, 0, 0, tiled=True)


def offer(ends, sides, tiles):
    channels = sides.shape[-1]
    half = sides.shape[0] // 2
    piece = 4 * half
    held = jnp.concatenate([ends[0], ends[ROWS - 1], sides], axis=0)
    order = jnp.arange(half)[:, None]
    order = jnp.concatenate(
        [order, half + order, 2 * half + 2 * order, 2 * half + 2 * order + 1], axis=1
    ).reshape(-1)
    everywhere = jnp.broadcast_to(order, (Z, piece)).reshape(-1)
    spread = take_rows(rows_of(everywhere, piece), held).reshape(Z, piece, channels)
    return spread, take_rows(rows_of(order[: piece // UNITS], piece), held)


def exchange(spread, first_own, tiles, plan, rider=None):
    lines = tiles * 4
    line, channels = first_own.shape
    piece = UNITS * line
    width = ROWS * line // lines
    gathered = lax.all_to_all(spread, "z", 0, 0, tiled=True).reshape(Z * piece, channels)
    sent = take_rows(plan["pick"], gathered).reshape(XH * CORE, -1, channels)
    arrived = lax.all_to_all(sent, COLUMN_AXES, 0, 0, tiled=True).reshape(-1, channels)
    mine = jnp.concatenate([take_rows(plan["select"], arrived), first_own], axis=0)
    count = mine.shape[0]
    mine = jnp.broadcast_to(mine[None], (ROWS,) + mine.shape)
    if rider is not None:
        mine = jnp.concatenate([mine, rider], axis=1)
    whole = lax.all_to_all(mine, ROW_AXES, 0, 0, tiled=True)
    first = whole[:, :line].reshape(ROWS * line, channels)
    second = whole[:, line : 2 * line].reshape(ROWS * line, channels)
    own = whole[:, piece + 4 * lines : count].reshape(ROWS * line, channels)
    corner = whole[:, piece : piece + 4 * lines].reshape(ROWS, 2, 2, lines, channels)
    corner = jnp.where(plan["finish"][:, None, :, None], corner[ROWS - 1], corner[0])
    corner = turn_channels(corner, plan["quarter_corner"][:, None])
    return (
        to_here(first, plan, "turned"),
        take_rows(plan["lines"], first).reshape(lines, width, channels),
        take_rows(plan["lines"], second).reshape(lines, width, channels),
        to_neighbour(own, plan, "turned"),
        corner,
        whole[:, count:],
    )


def by_side(cells, plan):
    blocks = [
        jnp.where((plan["side"] == side)[:, None, None], cells, jnp.zeros((), cells.dtype))
        for side in range(4)
    ]
    return jnp.concatenate(blocks, axis=-1)


def neighbour_edge(edge, inner, own, corner, kernel_weight, plan):
    width = own.shape[1]
    w = kernel_weight
    patch = [
        jnp.pad(own, ((0, 0), (1, 1), (0, 0))),
        jnp.concatenate([corner[0, 0][:, None], edge, corner[1, 0][:, None]], axis=1),
        jnp.concatenate([corner[0, 1][:, None], inner, corner[1, 1][:, None]], axis=1),
    ]
    total = None
    for depth in range(3):
        spread = by_side(patch[depth], plan)
        for tap in range(3):
            weights = jnp.concatenate(
                [w[depth, tap], w[2 - depth, tap], w[tap, depth], w[tap, 2 - depth]], axis=0
            )
            term = jnp.dot(spread[:, tap : tap + width], weights, preferred_element_type=f32)
            total = term if total is None else total + term
    return total, patch


def neighbour_border(grads, kernel_weight, plan):
    width = grads.shape[1]
    w = kernel_weight
    spread = by_side(jnp.pad(grads, ((0, 0), (1, 1), (0, 0))), plan)
    total = None
    for tap in range(3):
        weights = jnp.concatenate(
            [w[0, 2 - tap], w[2, 2 - tap], w[2 - tap, 0], w[2 - tap, 2]], axis=1
        )
        term = lax.dot_general(
            spread[:, tap : tap + width],
            weights,
            (((2,), (1,)), ((), ())),
            preferred_element_type=f32,
        )
        total = term if total is None else total + term
    return total


def own_part(lines, margin, plan):
    strip = lines.shape[1] // ROWS
    padded = jnp.pad(lines, ((0, 0), (margin, margin), (0, 0)))
    return lax.dynamic_slice_in_dim(padded, plan["row"] * strip, strip + 2 * margin, 1)


def with_ghosts(strips, ghosts, margin, plan):
    row = plan["row"]
    above = jnp.where(row == 0, ghosts[:, 0], strips[:, margin - 1])
    below = jnp.where(row == ROWS - 1, ghosts[:, 1], strips[:, -margin])
    middle = jnp.concatenate(
        [strips[:, : margin - 1], above[:, None], strips[:, margin:-margin], below[:, None]]
        + ([strips[:, -margin + 1 :]] if margin > 1 else []),
        axis=1,
    )
    left = own_part(ghosts[:, 2], margin, plan)
    right = own_part(ghosts[:, 3], margin, plan)
    return jnp.concatenate([left[:, :, None], middle, right[:, :, None]], axis=2)


def add_borders(interior, routed, margin, plan):
    row = plan["row"]
    routed = routed.astype(f32)
    rows = interior.shape[1]
    index = jnp.arange(rows)[None, :, None, None]
    top = jnp.where((row == 0) & (index == margin), routed[:, 0][:, None], 0.0)
    bottom = jnp.where(
        (row == ROWS - 1) & (index == rows - 1 - margin), routed[:, 1][:, None], 0.0
    )
    column = jnp.arange(interior.shape[2])[None, None, :, None]
    left = own_part(routed[:, 2], margin, plan)[:, :, None]
    right = own_part(routed[:, 3], margin, plan)[:, :, None]
    sides = jnp.where(column == 0, left, 0.0) + jnp.where(
        column == interior.shape[2] - 1, right, 0.0
    )
    return interior + top + bottom + sides


def inside(rows, margin, width, plan):
    strip = width // ROWS
    place = plan["row"] * strip - margin + jnp.arange(rows)
    return ((place >= 0) & (place < width))[None, :, None, None]


def convolve(padded, kernel_weight):
    rows = padded.shape[1] - 2
    columns = padded.shape[2] - 2
    total = None
    for row_tap in range(3):
        for col_tap in range(3):
            term = jnp.dot(
                padded[:, row_tap : row_tap + rows, col_tap : col_tap + columns],
                kernel_weight[row_tap, col_tap],
                preferred_element_type=f32,
            )
            total = term if total is None else total + term
    return total


def convolve_back(grads, kernel_weight, extra=0):
    rows = grads.shape[1] - 2
    columns = grads.shape[2] + extra
    grads = jnp.pad(grads, ((0, 0), (0, 0), (2, 2 + extra), (0, 0)))
    total = None
    for row_tap in range(3):
        for col_tap in range(3):
            term = lax.dot_general(
                grads[:, row_tap : row_tap + rows, col_tap : col_tap + columns + 2],
                kernel_weight[2 - row_tap, 2 - col_tap],
                (((3,), (1,)), ((), ())),
                preferred_element_type=f32,
            )
            total = term if total is None else total + term
    return total


def shifted(field, tap):
    return field.astype(f32)[tap : tap + field.shape[0] - 2].astype(field.dtype)


def strip_terms(padded_ref, grads_ref, out_ref, cells_ref, rows_ref):
    tiles, rows, columns = grads_ref.shape[:3]
    for row in range(rows + 2):
        for tile in range(tiles):
            at = (row * tiles + tile) * columns
            line = padded_ref[tile, row]
            for tap in range(3):
                cells_ref[tap, at : at + columns] = shifted(line, tap)
            if row < rows:
                rows_ref[at : at + columns] = grads_ref[tile, row]
    grads = rows_ref[...]
    step = tiles * columns
    for a in range(3):
        for b in range(3):
            out_ref[a * 3 + b] = lax.dot_general(
                cells_ref[b, a * step : (a + rows) * step],
                grads,
                (((0,), (0,)), ((), ())),
                preferred_element_type=f32,
            )


def border_terms(patch_ref, grads_ref, edges_ref, out_ref):
    depths, lines = patch_ref.shape[:2]
    width, channels = patch_ref.shape[2] - 2, patch_ref.shape[3]
    for depth in range(depths):
        for line in range(lines):
            cells = patch_ref[depth, line]
            for tap in range(3):
                edges_ref[tap, line * width : (line + 1) * width] = shifted(cells, tap)
        for tap in range(3):
            term = lax.dot_general(
                edges_ref[tap],
                grads_ref[...],
                (((0,), (0,)), ((), ())),
                preferred_element_type=f32,
            )
            places = ((depth, tap), (2 - depth, tap), (tap, depth), (tap, 2 - depth))
            for side, (a, b) in enumerate(places):
                out_ref[a * 3 + b] += term[:, side * channels : (side + 1) * channels]


def weight_grad(padded, grads, patch=None, edge_grads=None):
    tiles, rows, columns, channels = grads.shape
    scratch = [
        pltpu.VMEM((3, tiles * (rows + 2) * columns, channels), bf16),
        pltpu.VMEM((tiles * rows * columns, channels), bf16),
    ]
    operands = [padded, grads]
    if patch is None:
        kernel = strip_terms
    else:
        operands += [patch, edge_grads]
        scratch.append(pltpu.VMEM((3, edge_grads.shape[0], channels), bf16))

        def kernel(padded_ref, grads_ref, patch_ref, edge_ref, out_ref, cells, rows, edges):
            strip_terms(padded_ref, grads_ref, out_ref, cells, rows)
            border_terms(patch_ref, edge_ref, edges, out_ref)

    whole = pl.BlockSpec(memory_space=pltpu.VMEM)
    return pl.pallas_call(
        kernel,
        out_shape=jax.ShapeDtypeStruct((9, channels, channels), f32),
        in_specs=[whole] * len(operands),
        out_specs=whole,
        scratch_shapes=scratch,
        compiler_params=pltpu.CompilerParams(vmem_limit_bytes=40 * 2**20),
        cost_estimate=pl.CostEstimate(flops=1000, bytes_accessed=1000, transcendentals=0),
    )(*operands)


def grouped_cells(field):
    tiles, rows, columns, channels = field.shape
    return field.reshape(tiles, rows // 2, 2, columns // 2, 2, channels)


def strided_shrink(field, kernel_weight):
    grouped = grouped_cells(field)
    total = None
    for row_tap in range(2):
        for col_tap in range(2):
            term = jnp.dot(
                grouped[:, :, row_tap, :, col_tap],
                kernel_weight[row_tap, col_tap],
                preferred_element_type=f32,
            )
            total = term if total is None else total + term
    return total


def upsample_back(grads, kernel_weight):
    tiles, rows, columns, channels = grads.shape
    stacked = []
    for row_tap in range(2):
        pieces = [
            lax.dot_general(
                grads,
                kernel_weight[row_tap, col_tap],
                (((3,), (1,)), ((), ())),
                preferred_element_type=f32,
            )
            for col_tap in range(2)
        ]
        stacked.append(jnp.stack(pieces, axis=3))
    return jnp.stack(stacked, axis=2).reshape(tiles, rows * 2, columns * 2, kernel_weight.shape[2])


def down_grad(field, grads):
    grouped = grouped_cells(field)
    return jnp.stack([
        lax.dot_general(
            grouped[:, :, row_tap, :, col_tap],
            grads,
            (((0, 1, 2), (0, 1, 2)), ((), ())),
            preferred_element_type=f32,
        )
        for row_tap in range(2)
        for col_tap in range(2)
    ])


def silu(value):
    return value * jax.nn.sigmoid(value)


def silu_slope(value):
    sigma = jax.nn.sigmoid(value)
    return sigma * (1.0 + value * (1.0 - sigma))


SWAP = [(0, 1), (1, 0)]


def sum_pair(blocks):
    channels = blocks[0].shape[-1]
    core = lax.axis_index("c")
    rows = jnp.concatenate([block.reshape(-1, channels) for block in blocks], axis=0)
    first, second = rows[: rows.shape[0] // 2], rows[rows.shape[0] // 2 :]
    sent = jnp.where(core == 0, second, first).astype(bf16)
    held = jnp.where(core == 0, first, second) + lax.ppermute(sent, "c", SWAP).astype(f32)
    return held.astype(bf16).reshape(ROWS, -1, channels)


def sum_rest(held, factor):
    channels = held.shape[-1]
    core = lax.axis_index("c")
    held = held.astype(f32).sum(0)
    held = held.astype(bf16).reshape(XH * Z, -1, channels)
    held = lax.all_to_all(held, ("xh", "z"), 0, 0, tiled=True).astype(f32).sum(0)
    held = (held * factor).astype(bf16)
    held = broadcast_all(held, ("xh", "z"), XH * Z).reshape(-1, channels)
    held = broadcast_all(held, ROW_AXES, ROWS).reshape(-1, channels)
    other = lax.ppermute(held, "c", SWAP)
    first = jnp.where(core == 0, held, other)
    second = jnp.where(core == 0, other, held)
    return jnp.concatenate([first, second], axis=0).astype(f32).reshape(-1, channels, channels)


def body(activations, matching, first_kernel_weight, conv_second, reduce_kernel_weight, cotangent):
    tiles, strip, width, channels = activations.shape
    factor = 1.0 / math.sqrt(matching.shape[0] * width * width)

    first_rows = jnp.concatenate(
        [activations[:, :4].reshape(tiles, 4 * width, channels), cotangent[:, 0]], axis=1
    )
    last_rows = jnp.concatenate(
        [activations[:, -4:].reshape(tiles, 4 * width, channels), cotangent[:, -1]], axis=1
    )
    def sides_of(lines):
        return lines.reshape(tiles, 4, width, channels)

    ends, sides = outer_lines(activations, 0, lax.axis_index(ROW_AXES))
    pieces, first_own = offer(share_ends(ends), sides, tiles)
    pieces, first_rows, last_rows, matching = lax.optimization_barrier(
        (pieces, first_rows, last_rows, matching)
    )
    plan = routing(matching, strip)
    ghosts, edge, inner, own, corner, _ = exchange(pieces, first_own, tiles, plan)
    above = lax.ppermute(last_rows, ROW_AXES, [(i, i + 1) for i in range(ROWS - 1)])
    below = lax.ppermute(first_rows, ROW_AXES, [(i + 1, i) for i in range(ROWS - 1)])
    cells = 4 * width
    wide_input = jnp.concatenate(
        [
            above[:, :cells].reshape(tiles, 4, width, channels),
            activations,
            below[:, :cells].reshape(tiles, 4, width, channels),
        ],
        axis=1,
    )
    wide_cotangent = jnp.concatenate(
        [above[:, None, cells:], cotangent, below[:, None, cells:]], axis=1
    )

    edge_first, edge_cells = neighbour_edge(edge, inner, own, corner, first_kernel_weight, plan)
    padded_input = with_ghosts(wide_input, sides_of(ghosts), 4, plan)
    pre_first = convolve(padded_input, first_kernel_weight)
    hidden_first = jnp.where(
        inside(strip + 6, 3, width, plan), silu(pre_first).astype(bf16), jnp.zeros((), bf16)
    )

    ghosts = sides_of(to_here(silu(edge_first).astype(bf16), plan))
    padded_hidden = with_ghosts(hidden_first, ghosts, 3, plan)
    pre_second = convolve(padded_hidden, conv_second)
    hidden_second = silu(pre_second[:, 2:-2]).astype(bf16)
    output = strided_shrink(hidden_second, reduce_kernel_weight).astype(bf16)
    grad_second = (
        upsample_back(wide_cotangent, reduce_kernel_weight) * silu_slope(pre_second)
    ).astype(bf16)

    spread = convolve_back(grad_second, conv_second, EXTRA)
    narrow = spread.astype(bf16)
    ends, sides = outer_lines(narrow, 1, plan["row"])
    pieces, first_own = offer(share_ends(ends), sides, tiles)
    pieces, held_spread, held_narrow = lax.optimization_barrier((pieces, spread, narrow))

    edge_slope = silu_slope(edge_first)
    slope_first = silu_slope(pre_first[:, 2:-2])
    own_grad = (held_spread[:, 1:-1, 1 : width + 1] * slope_first[:, 1:-1]).astype(bf16)
    border_grad = (own_borders(held_narrow, plan).astype(f32) * edge_slope).astype(bf16)
    edge_grad = by_side(border_grad, plan).reshape(tiles * 4 * width, 4 * channels)
    parts = sum_pair(
        [
            weight_grad(padded_input[:, 3:-3], own_grad, jnp.stack(edge_cells), edge_grad),
            weight_grad(padded_hidden[:, 2:-2], grad_second[:, 2:-2]),
            down_grad(hidden_second, cotangent),
        ]
    )

    routed, _, inner, own, corner, parts = exchange(
        pieces, first_own, tiles, plan, parts
    )
    routed = sides_of(routed)
    grad_first_hidden = add_borders(spread[:, :, 1 : width + 1], routed, 1, plan)
    grad_first = jnp.where(
        inside(strip + 2, 1, width, plan),
        (grad_first_hidden * slope_first).astype(bf16),
        jnp.zeros((), bf16),
    )

    place = jnp.arange(width)[None, :, None]
    corner = corner.astype(f32)
    edge_hidden = (
        inner.astype(f32)
        + own.astype(f32)
        + jnp.where(place == 0, corner[0, 0][:, None], 0.0)
        + jnp.where(place == width - 1, corner[1, 0][:, None], 0.0)
    )
    edge_grad = (edge_hidden * edge_slope).astype(bf16)
    routed = sides_of(to_here(neighbour_border(edge_grad, first_kernel_weight, plan).astype(bf16), plan))
    spread = convolve_back(grad_first, first_kernel_weight)
    grad_activations = add_borders(spread[:, :, 1:-1], routed, 0, plan).astype(bf16)

    summed = sum_rest(parts, factor)
    square = (channels, channels)
    return (
        output,
        grad_activations,
        summed[:9].reshape((3, 3) + square),
        summed[9:18].reshape((3, 3) + square),
        summed[18:].reshape((2, 2) + square),
    )


def solution(mesh):
    fine = Mesh(mesh.devices.reshape(XH, Z, CORE, Y, XL), TILE_AXES + ROW_AXES)
    placed = P(TILE_AXES, ROW_AXES, None, None)
    return jax.shard_map(
        body,
        mesh=fine,
        in_specs=(placed, P(), P(), P(), P(), placed),
        out_specs=(placed, placed, P(), P(), P()),
        check_vma=False,
    )
```

```python
import functools
import math

import jax
import jax.numpy as jnp
import numpy as np
from jax import lax
from jax.experimental import pallas as pl
from jax.experimental.pallas import tpu as pltpu
from jax.sharding import Mesh, PartitionSpec as P

XH, Z, CORE, Y, XL = 2, 8, 2, 4, 2
ROWS = Y * XL
UNITS = 2
EXTRA = 14
TILE_AXES = ("xh", "z", "c")
ROW_AXES = ("y", "xl")
COLUMN_AXES = ("xh", "c")
f32 = jnp.float32
bf16 = jnp.bfloat16


def broadcast_all(piece, axes, count):
    return lax.all_to_all(
        jnp.broadcast_to(piece[None], (count,) + piece.shape), axes, 0, 0, tiled=True
    )


def column_of(group):
    return (group // (Z * CORE)) * CORE + group % CORE


def routing(matching, strip):
    tiles = matching.shape[0]
    here = tiles // (XH * Z * CORE)
    lines = here * 4
    xh, z, core = lax.axis_index("xh"), lax.axis_index("z"), lax.axis_index("c")
    me = xh * CORE + core
    sides = matching.reshape(tiles * 4, 4)
    grouped = matching.reshape(XH, Z, CORE, lines, 4)
    column = lax.dynamic_index_in_dim(grouped, z, 1, keepdims=False).reshape(XH * CORE * lines, 4)
    tile, side = column[:, 0], column[:, 1]
    beside = jnp.where(side < 2, 2, 0)[:, None] + jnp.arange(2)[None, :]
    corners = sides[tile[:, None] * 4 + beside]
    finish = (side[:, None] % 2) ^ corners[..., 2]

    row = lax.axis_index(ROW_AXES)
    cells = UNITS * strip
    piece = cells * lines
    width = ROWS * strip

    def place(tile, side):
        group = tile // here
        held = column_of(group) == me
        return held, ((group // CORE) % Z) * piece + (tile % here) * 4 + side

    def own(table):
        return lax.dynamic_slice_in_dim(table, me * lines, lines, 0)

    held, at = place(tile, side)
    columns = XH * CORE
    cell = np.arange(cells, dtype=np.int32)[None, :, None] * lines
    pick = jnp.where(held.reshape(columns, 1, lines), at.reshape(columns, 1, lines) + cell, -1)
    held, at = place(corners[..., 0], corners[..., 1])
    at = jnp.where(held, at, -Z * piece).reshape(columns, lines, 2).swapaxes(1, 2)
    depth = np.array([0, 1, 0, 1], np.int32)
    depth = jnp.where(row == 0, depth, strip - 1 - depth)[None, :, None] * lines
    pick = jnp.concatenate([pick, jnp.repeat(at, 2, axis=1) + depth], axis=1).reshape(-1)

    mine, my_corners = own(column), own(corners)
    sent = piece + 4 * lines
    source = column_of(mine[:, 0] // here)[None, :]
    source_corner = column_of(my_corners[..., 0] // here).T
    select = jnp.concatenate(
        [jnp.broadcast_to(source, (cells, lines)), jnp.repeat(source_corner, 2, axis=0)], axis=0
    ).reshape(-1) * sent + np.arange(sent, dtype=np.int32)

    flipped = jnp.broadcast_to(mine[:, 2:3] == 1, (lines, width)).reshape(-1)
    position = np.arange(width, dtype=np.int32)[None, :]
    line = np.arange(lines, dtype=np.int32)[:, None]
    count = lines * width

    def places(position, step, base):
        return (position * step + line * base).reshape(-1)

    turned = jnp.where(
        flipped, places(width - 1 - position, lines, 1), places(position, lines, 1)
    )
    flip = jnp.where(flipped, places(width - 1 - position, 1, width), places(position, 1, width))
    return {
        "pick": rows_of(pick, Z * piece),
        "select": rows_of(select, columns * sent),
        "lines": rows_of(places(position, lines, 1), count),
        "turned": rows_of(turned, count),
        "flip": rows_of(flip, count),
        "flipped": flipped,
        "side": mine[:, 1],
        "quarter": mine[:, 3],
        "quarter_corner": my_corners[..., 3].T,
        "finish": own(finish).T == 1,
        "row": row,
    }


def rows_of(index, count):
    return (index[:, None] == jnp.arange(count)[None, :]).astype(bf16)


def take_rows(choice, rows):
    return jnp.dot(choice, rows, preferred_element_type=f32).astype(bf16)


def turn_channels(lines, quarter):
    half = lines.shape[-1] // 2
    first, second = lines[..., :half], lines[..., half:]
    quarter = quarter.reshape(quarter.shape + (1,) * (lines.ndim - quarter.ndim))
    odd = quarter % 2 == 1
    lead = jnp.where(odd, second, first)
    trail = jnp.where(odd, first, second)
    lead = jnp.where((quarter == 1) | (quarter == 2), -lead, lead)
    trail = jnp.where((quarter == 2) | (quarter == 3), -trail, trail)
    return jnp.concatenate([lead, trail], axis=-1)


def to_here(lines, plan, order="flip"):
    sides = plan["quarter"].shape[0]
    rows = take_rows(plan[order], lines.reshape(-1, lines.shape[-1]))
    return turn_channels(rows.reshape(sides, -1, lines.shape[-1]), plan["quarter"])


def to_neighbour(lines, plan, order="flip"):
    sides = plan["quarter"].shape[0]
    rows = take_rows(plan[order], lines.reshape(-1, lines.shape[-1]))
    return turn_channels(rows.reshape(sides, -1, lines.shape[-1]), (4 - plan["quarter"]) % 4)


def outer_lines(field, margin, row):
    tiles, rows, columns, channels = field.shape
    strip = rows - 2 * margin
    width = ROWS * strip
    unit = np.arange(UNITS)[:, None, None]
    cell = np.arange(strip)[None, :, None]
    tile = np.arange(tiles)[None, None, :] * (rows * columns)
    target = np.arange(ROWS)[:, None, None, None]
    last = width + 2 * margin - 1
    sides = np.stack([unit + tile, last - unit + tile], axis=-1) + (margin + cell)[..., None] * columns

    def index_of(line):
        ends = tile + line * columns + margin + target * strip + cell
        return np.concatenate([ends.reshape(-1), sides.reshape(-1)]).astype(np.int32)

    index = jnp.where(row == ROWS - 1, index_of(rows - 1 - unit), index_of(unit))
    chosen = take_rows(rows_of(index, tiles * rows * columns), field.reshape(-1, channels))
    cut = ROWS * UNITS * strip * tiles
    return chosen[:cut].reshape(ROWS, -1, channels), chosen[cut:]


def own_borders(field, plan):
    tiles, rows, columns, channels = field.shape
    strip = rows - 2
    width = ROWS * strip
    row = plan["row"]
    side = np.arange(4)[None, :, None]
    tile = np.arange(tiles)[:, None, None] * (rows * columns)

    def places(at):
        end = np.where(side == 0, 1 + at, (rows - 1) * columns + 1 + at)
        along = (1 + at) * columns + np.where(side == 2, 0, width + 1)
        index = tile + np.where(side < 2, end, along)
        owner = np.where(side < 2, side * (ROWS - 1), at // strip) + 0 * tile
        return index.reshape(-1).astype(np.int32), owner.reshape(-1).astype(np.int32)

    at = np.arange(width)[None, None, :]
    straight, owner = places(at)
    turned, owner_turned = places(width - 1 - at)
    index = jnp.where(plan["flipped"], turned, straight)
    off = np.where(side < 2, 0, strip * columns) + 0 * tile + 0 * at
    index = index - row * off.reshape(-1).astype(np.int32)
    index = jnp.where(jnp.where(plan["flipped"], owner_turned, owner) == row, index, -1)
    chosen = take_rows(rows_of(index, tiles * rows * columns), field.reshape(-1, channels))
    return turn_channels(chosen.reshape(tiles * 4, width, channels), (4 - plan["quarter"]) % 4)


def share_ends(ends):
    return lax.all_to_all(ends, ROW_AXES, 0, 0, tiled=True)


def offer(ends, sides, tiles):
    channels = sides.shape[-1]
    half = sides.shape[0] // 2
    piece = 4 * half
    held = jnp.concatenate([ends[0], ends[ROWS - 1], sides], axis=0)
    order = np.arange(half, dtype=np.int32)[:, None]
    order = np.concatenate(
        [order, half + order, 2 * half + 2 * order, 2 * half + 2 * order + 1], axis=1
    ).reshape(-1)
    everywhere = np.tile(order, Z)
    spread = take_rows(rows_of(everywhere, piece), held).reshape(Z, piece, channels)
    return spread, take_rows(rows_of(order[: piece // UNITS], piece), held)


def exchange(spread, first_own, tiles, plan, rider=None):
    lines = tiles * 4
    line, channels = first_own.shape
    piece = UNITS * line
    width = ROWS * line // lines
    gathered = lax.all_to_all(spread, "z", 0, 0, tiled=True).reshape(Z * piece, channels)
    sent = take_rows(plan["pick"], gathered).reshape(XH * CORE, -1, channels)
    arrived = lax.all_to_all(sent, COLUMN_AXES, 0, 0, tiled=True).reshape(-1, channels)
    mine = jnp.concatenate([take_rows(plan["select"], arrived), first_own], axis=0)
    count = mine.shape[0]
    mine = jnp.broadcast_to(mine[None], (ROWS,) + mine.shape)
    if rider is not None:
        mine = jnp.concatenate([mine, rider], axis=1)
    whole = lax.all_to_all(mine, ROW_AXES, 0, 0, tiled=True)
    first = whole[:, :line].reshape(ROWS * line, channels)
    second = whole[:, line : 2 * line].reshape(ROWS * line, channels)
    own = whole[:, piece + 4 * lines : count].reshape(ROWS * line, channels)
    corner = whole[:, piece : piece + 4 * lines].reshape(ROWS, 2, 2, lines, channels)
    corner = jnp.where(plan["finish"][:, None, :, None], corner[ROWS - 1], corner[0])
    corner = turn_channels(corner, plan["quarter_corner"][:, None])
    return (
        to_here(first, plan, "turned"),
        take_rows(plan["lines"], first).reshape(lines, width, channels),
        take_rows(plan["lines"], second).reshape(lines, width, channels),
        to_neighbour(own, plan, "turned"),
        corner,
        whole[:, count:],
    )


def by_side(cells, plan):
    blocks = [
        jnp.where((plan["side"] == side)[:, None, None], cells, jnp.zeros((), cells.dtype))
        for side in range(4)
    ]
    return jnp.concatenate(blocks, axis=-1)


def neighbour_edge(edge, inner, own, corner, kernel_weight, plan):
    width = own.shape[1]
    w = kernel_weight
    patch = [
        jnp.pad(own, ((0, 0), (1, 1), (0, 0))),
        jnp.concatenate([corner[0, 0][:, None], edge, corner[1, 0][:, None]], axis=1),
        jnp.concatenate([corner[0, 1][:, None], inner, corner[1, 1][:, None]], axis=1),
    ]
    total = None
    for depth in range(3):
        spread = by_side(patch[depth], plan)
        for tap in range(3):
            weights = jnp.concatenate(
                [w[depth, tap], w[2 - depth, tap], w[tap, depth], w[tap, 2 - depth]], axis=0
            )
            term = jnp.dot(spread[:, tap : tap + width], weights, preferred_element_type=f32)
            total = term if total is None else total + term
    return total, patch


def neighbour_border(grads, kernel_weight, plan):
    width = grads.shape[1]
    w = kernel_weight
    spread = by_side(jnp.pad(grads, ((0, 0), (1, 1), (0, 0))), plan)
    total = None
    for tap in range(3):
        weights = jnp.concatenate(
            [w[0, 2 - tap], w[2, 2 - tap], w[2 - tap, 0], w[2 - tap, 2]], axis=1
        )
        term = lax.dot_general(
            spread[:, tap : tap + width],
            weights,
            (((2,), (1,)), ((), ())),
            preferred_element_type=f32,
        )
        total = term if total is None else total + term
    return total


def own_part(lines, margin, plan):
    strip = lines.shape[1] // ROWS
    padded = jnp.pad(lines, ((0, 0), (margin, margin), (0, 0)))
    return lax.dynamic_slice_in_dim(padded, plan["row"] * strip, strip + 2 * margin, 1)


def with_ghosts(strips, ghosts, margin, plan):
    row = plan["row"]
    above = jnp.where(row == 0, ghosts[:, 0], strips[:, margin - 1])
    below = jnp.where(row == ROWS - 1, ghosts[:, 1], strips[:, -margin])
    middle = jnp.concatenate(
        [strips[:, : margin - 1], above[:, None], strips[:, margin:-margin], below[:, None]]
        + ([strips[:, -margin + 1 :]] if margin > 1 else []),
        axis=1,
    )
    left = own_part(ghosts[:, 2], margin, plan)
    right = own_part(ghosts[:, 3], margin, plan)
    return jnp.concatenate([left[:, :, None], middle, right[:, :, None]], axis=2)


def add_borders(interior, routed, margin, plan):
    row = plan["row"]
    routed = routed.astype(f32)
    rows = interior.shape[1]
    index = jnp.arange(rows)[None, :, None, None]
    top = jnp.where((row == 0) & (index == margin), routed[:, 0][:, None], 0.0)
    bottom = jnp.where(
        (row == ROWS - 1) & (index == rows - 1 - margin), routed[:, 1][:, None], 0.0
    )
    column = jnp.arange(interior.shape[2])[None, None, :, None]
    left = own_part(routed[:, 2], margin, plan)[:, :, None]
    right = own_part(routed[:, 3], margin, plan)[:, :, None]
    sides = jnp.where(column == 0, left, 0.0) + jnp.where(
        column == interior.shape[2] - 1, right, 0.0
    )
    return interior + top + bottom + sides


def inside(rows, margin, width, plan):
    strip = width // ROWS
    place = plan["row"] * strip - margin + jnp.arange(rows)
    return ((place >= 0) & (place < width))[None, :, None, None]


def shifted(field, tap):
    return field.astype(f32)[tap : tap + field.shape[0] - 2].astype(field.dtype)


def convolve_cells(back, padded_ref, weight_ref, out_ref, cells_ref):
    tiles, rows, columns = out_ref.shape[:3]
    step = tiles * columns
    for row in range(rows + 2):
        for tile in range(tiles):
            at = row * step + tile * columns
            line = padded_ref[tile, row]
            for tap in range(3):
                cells_ref[tap, at : at + columns] = shifted(line, tap)
    for row in range(0, rows, 2):
        total = None
        for a in range(3):
            for b in range(3):
                cells = cells_ref[b, (row + a) * step : (row + a + 2) * step]
                weight = weight_ref[2 - a, 2 - b] if back else weight_ref[a, b]
                term = lax.dot_general(
                    cells,
                    weight,
                    (((1,), (1 if back else 0,)), ((), ())),
                    preferred_element_type=f32,
                )
                total = term if total is None else total + term
        for half in range(2):
            for tile in range(tiles):
                at = half * step + tile * columns
                out_ref[tile, row + half] = total[at : at + columns]


WHOLE = pl.BlockSpec(memory_space=pltpu.VMEM)
ROOM = pltpu.CompilerParams(vmem_limit_bytes=40 * 2**20)
CHEAP = pl.CostEstimate(flops=1000, bytes_accessed=1000, transcendentals=0)


def convolve(padded, kernel_weight, back=False):
    tiles, rows, columns, channels = padded.shape
    return pl.pallas_call(
        functools.partial(convolve_cells, back),
        out_shape=jax.ShapeDtypeStruct((tiles, rows - 2, columns - 2, channels), f32),
        in_specs=[WHOLE] * 2,
        out_specs=WHOLE,
        scratch_shapes=[pltpu.VMEM((3, tiles * rows * (columns - 2), channels), bf16)],
        compiler_params=ROOM,
        cost_estimate=CHEAP,
    )(padded, kernel_weight)


def with_columns(grads, before, after):
    return jnp.pad(grads, ((0, 0), (0, 0), (before, after), (0, 0)))


def strip_terms(padded_ref, grads_ref, out_ref, cells_ref, rows_ref):
    tiles, rows, columns = grads_ref.shape[:3]
    for row in range(rows + 2):
        for tile in range(tiles):
            at = (row * tiles + tile) * columns
            line = padded_ref[tile, row]
            for tap in range(3):
                cells_ref[tap, at : at + columns] = shifted(line, tap)
            if row < rows:
                rows_ref[at : at + columns] = grads_ref[tile, row]
    grads = rows_ref[...]
    step = tiles * columns
    for a in range(3):
        for b in range(3):
            out_ref[a * 3 + b] = lax.dot_general(
                cells_ref[b, a * step : (a + rows) * step],
                grads,
                (((0,), (0,)), ((), ())),
                preferred_element_type=f32,
            )


def border_terms(patch_ref, grads_ref, edges_ref, out_ref):
    depths, lines = patch_ref.shape[:2]
    width, channels = patch_ref.shape[2] - 2, patch_ref.shape[3]
    for depth in range(depths):
        for line in range(lines):
            cells = patch_ref[depth, line]
            for tap in range(3):
                edges_ref[tap, line * width : (line + 1) * width] = shifted(cells, tap)
        for tap in range(3):
            term = lax.dot_general(
                edges_ref[tap],
                grads_ref[...],
                (((0,), (0,)), ((), ())),
                preferred_element_type=f32,
            )
            places = ((depth, tap), (2 - depth, tap), (tap, depth), (tap, 2 - depth))
            for side, (a, b) in enumerate(places):
                out_ref[a * 3 + b] += term[:, side * channels : (side + 1) * channels]


def weight_grad(padded, grads, patch=None, edge_grads=None):
    tiles, rows, columns, channels = grads.shape
    scratch = [
        pltpu.VMEM((3, tiles * (rows + 2) * columns, channels), bf16),
        pltpu.VMEM((tiles * rows * columns, channels), bf16),
    ]
    operands = [padded, grads]
    if patch is None:
        kernel = strip_terms
    else:
        operands += [patch, edge_grads]
        scratch.append(pltpu.VMEM((3, edge_grads.shape[0], channels), bf16))

        def kernel(padded_ref, grads_ref, patch_ref, edge_ref, out_ref, cells, rows, edges):
            strip_terms(padded_ref, grads_ref, out_ref, cells, rows)
            border_terms(patch_ref, edge_ref, edges, out_ref)

    return pl.pallas_call(
        kernel,
        out_shape=jax.ShapeDtypeStruct((9, channels, channels), f32),
        in_specs=[WHOLE] * len(operands),
        out_specs=WHOLE,
        scratch_shapes=scratch,
        compiler_params=ROOM,
        cost_estimate=CHEAP,
    )(*operands)


def grouped_cells(field):
    tiles, rows, columns, channels = field.shape
    return field.reshape(tiles, rows // 2, 2, columns // 2, 2, channels)


def strided_shrink(field, kernel_weight):
    grouped = grouped_cells(field)
    total = None
    for row_tap in range(2):
        for col_tap in range(2):
            term = jnp.dot(
                grouped[:, :, row_tap, :, col_tap],
                kernel_weight[row_tap, col_tap],
                preferred_element_type=f32,
            )
            total = term if total is None else total + term
    return total


def upsample_back(grads, kernel_weight):
    tiles, rows, columns, channels = grads.shape
    stacked = []
    for row_tap in range(2):
        pieces = [
            lax.dot_general(
                grads,
                kernel_weight[row_tap, col_tap],
                (((3,), (1,)), ((), ())),
                preferred_element_type=f32,
            )
            for col_tap in range(2)
        ]
        stacked.append(jnp.stack(pieces, axis=3))
    return jnp.stack(stacked, axis=2).reshape(tiles, rows * 2, columns * 2, kernel_weight.shape[2])


def down_terms(cells_ref, grads_ref, out_ref):
    for tap in range(cells_ref.shape[0]):
        out_ref[tap] = lax.dot_general(
            cells_ref[tap],
            grads_ref[...],
            (((0,), (0,)), ((), ())),
            preferred_element_type=f32,
        )


def down_grad(field, grads):
    channels = field.shape[-1]
    cells = grouped_cells(field).transpose(2, 4, 0, 1, 3, 5).reshape(4, -1, channels)
    return pl.pallas_call(
        down_terms,
        out_shape=jax.ShapeDtypeStruct((4, channels, channels), f32),
        in_specs=[WHOLE] * 2,
        out_specs=WHOLE,
        compiler_params=ROOM,
        cost_estimate=CHEAP,
    )(cells, grads.reshape(-1, channels))


def silu(value):
    return value * jax.nn.sigmoid(value)


def silu_slope(value):
    sigma = jax.nn.sigmoid(value)
    return sigma * (1.0 + value * (1.0 - sigma))


SWAP = [(0, 1), (1, 0)]


def sum_pair(blocks):
    channels = blocks[0].shape[-1]
    core = lax.axis_index("c")
    rows = jnp.concatenate([block.reshape(-1, channels) for block in blocks], axis=0)
    first, second = rows[: rows.shape[0] // 2], rows[rows.shape[0] // 2 :]
    sent = jnp.where(core == 0, second, first).astype(bf16)
    held = jnp.where(core == 0, first, second) + lax.ppermute(sent, "c", SWAP).astype(f32)
    return held.astype(bf16).reshape(ROWS, -1, channels)


def sum_shards(held, factor):
    channels = held.shape[-1]
    held = held.astype(f32).sum(0)
    held = held.astype(bf16).reshape(XH * Z, -1, channels)
    held = lax.all_to_all(held, ("xh", "z"), 0, 0, tiled=True).astype(f32).sum(0)
    held = (held * factor).astype(bf16)
    return broadcast_all(held, ("xh", "z"), XH * Z).reshape(-1, channels)


def gather_sums(held, beside):
    channels = held.shape[-1]
    core = lax.axis_index("c")
    held = broadcast_all(held, ROW_AXES, ROWS).reshape(-1, channels)
    held, beside = lax.optimization_barrier((held, beside))
    other = lax.ppermute(held, "c", SWAP)
    first = jnp.where(core == 0, held, other)
    second = jnp.where(core == 0, other, held)
    both = jnp.concatenate([first, second], axis=0).astype(f32)
    return both.reshape(-1, channels, channels), beside


def body(activations, matching, first_kernel_weight, conv_second, reduce_kernel_weight, cotangent):
    tiles, strip, width, channels = activations.shape
    factor = 1.0 / math.sqrt(matching.shape[0] * width * width)

    first_rows = jnp.concatenate(
        [activations[:, :4].reshape(tiles, 4 * width, channels), cotangent[:, 0]], axis=1
    )
    last_rows = jnp.concatenate(
        [activations[:, -4:].reshape(tiles, 4 * width, channels), cotangent[:, -1]], axis=1
    )
    def sides_of(lines):
        return lines.reshape(tiles, 4, width, channels)

    ends, sides = outer_lines(activations, 0, lax.axis_index(ROW_AXES))
    pieces, first_own = offer(share_ends(ends), sides, tiles)
    pieces, first_rows, last_rows, matching = lax.optimization_barrier(
        (pieces, first_rows, last_rows, matching)
    )
    plan = routing(matching, strip)
    ghosts, edge, inner, own, corner, _ = exchange(pieces, first_own, tiles, plan)
    above = lax.ppermute(last_rows, ROW_AXES, [(i, i + 1) for i in range(ROWS - 1)])
    below = lax.ppermute(first_rows, ROW_AXES, [(i + 1, i) for i in range(ROWS - 1)])
    cells = 4 * width
    wide_input = jnp.concatenate(
        [
            above[:, :cells].reshape(tiles, 4, width, channels),
            activations,
            below[:, :cells].reshape(tiles, 4, width, channels),
        ],
        axis=1,
    )
    wide_cotangent = jnp.concatenate(
        [above[:, None, cells:], cotangent, below[:, None, cells:]], axis=1
    )

    edge_first, edge_cells = neighbour_edge(edge, inner, own, corner, first_kernel_weight, plan)
    padded_input = with_ghosts(wide_input, sides_of(ghosts), 4, plan)
    pre_first = convolve(padded_input, first_kernel_weight)
    hidden_first = jnp.where(
        inside(strip + 6, 3, width, plan), silu(pre_first).astype(bf16), jnp.zeros((), bf16)
    )

    ghosts = sides_of(to_here(silu(edge_first).astype(bf16), plan))
    padded_hidden = with_ghosts(hidden_first, ghosts, 3, plan)
    pre_second = convolve(padded_hidden, conv_second)
    hidden_second = silu(pre_second[:, 2:-2]).astype(bf16)
    output = strided_shrink(hidden_second, reduce_kernel_weight).astype(bf16)
    grad_second = (
        upsample_back(wide_cotangent, reduce_kernel_weight) * silu_slope(pre_second)
    ).astype(bf16)

    spread = convolve(with_columns(grad_second, 2, 2 + EXTRA), conv_second, True)
    narrow = spread.astype(bf16)
    ends, sides = outer_lines(narrow, 1, plan["row"])
    pieces, first_own = offer(share_ends(ends), sides, tiles)
    pieces, held_spread, held_narrow = lax.optimization_barrier((pieces, spread, narrow))

    edge_slope = silu_slope(edge_first)
    slope_first = silu_slope(pre_first[:, 2:-2])
    own_grad = (held_spread[:, 1:-1, 1 : width + 1] * slope_first[:, 1:-1]).astype(bf16)
    border_grad = (own_borders(held_narrow, plan).astype(f32) * edge_slope).astype(bf16)
    edge_grad = by_side(border_grad, plan).reshape(tiles * 4 * width, 4 * channels)
    parts = sum_pair(
        [
            weight_grad(padded_input[:, 3:-3], own_grad, jnp.stack(edge_cells), edge_grad),
            weight_grad(padded_hidden[:, 2:-2], grad_second[:, 2:-2]),
            down_grad(hidden_second, cotangent),
        ]
    )

    routed, _, inner, own, corner, parts = exchange(
        pieces, first_own, tiles, plan, parts
    )
    routed = sides_of(routed)
    grad_first_hidden = add_borders(spread[:, :, 1 : width + 1], routed, 1, plan)
    grad_first = jnp.where(
        inside(strip + 2, 1, width, plan),
        (grad_first_hidden * slope_first).astype(bf16),
        jnp.zeros((), bf16),
    )

    place = jnp.arange(width)[None, :, None]
    corner = corner.astype(f32)
    edge_hidden = (
        inner.astype(f32)
        + own.astype(f32)
        + jnp.where(place == 0, corner[0, 0][:, None], 0.0)
        + jnp.where(place == width - 1, corner[1, 0][:, None], 0.0)
    )
    edge_grad = (edge_hidden * edge_slope).astype(bf16)
    routed = sides_of(to_here(neighbour_border(edge_grad, first_kernel_weight, plan).astype(bf16), plan))
    spread = convolve(with_columns(grad_first, 1, 1), first_kernel_weight, True)
    shards, spread = lax.optimization_barrier((sum_shards(parts, factor), spread))
    grad_activations = add_borders(spread, routed, 0, plan).astype(bf16)
    summed, (output, grad_activations) = gather_sums(shards, (output, grad_activations))
    square = (channels, channels)
    return (
        output,
        grad_activations,
        summed[:9].reshape((3, 3) + square),
        summed[9:18].reshape((3, 3) + square),
        summed[18:].reshape((2, 2) + square),
    )


def solution(mesh):
    fine = Mesh(mesh.devices.reshape(XH, Z, CORE, Y, XL), TILE_AXES + ROW_AXES)
    placed = P(TILE_AXES, ROW_AXES, None, None)
    return jax.shard_map(
        body,
        mesh=fine,
        in_specs=(placed, P(), P(), P(), P(), placed),
        out_specs=(placed, placed, P(), P(), P()),
        check_vma=False,
    )
```

```python
import functools
import math

import jax
import jax.numpy as jnp
import numpy as np
from jax import lax
from jax.experimental import pallas as pl
from jax.experimental.pallas import tpu as pltpu
from jax.sharding import Mesh, PartitionSpec as P

XH, Z, CORE, Y, XL = 2, 8, 2, 4, 2
ROWS = Y * XL
UNITS = 2
EXTRA = 14
TILE_AXES = ("xh", "z", "c")
ROW_AXES = ("y", "xl")
COLUMN_AXES = ("xh", "c")
f32 = jnp.float32
bf16 = jnp.bfloat16


def broadcast_all(piece, axes, count):
    return lax.all_to_all(
        jnp.broadcast_to(piece[None], (count,) + piece.shape), axes, 0, 0, tiled=True
    )


def column_of(group):
    return (group // (Z * CORE)) * CORE + group % CORE


def routing(matching, strip, channels):
    tiles = matching.shape[0]
    here = tiles // (XH * Z * CORE)
    lines = here * 4
    xh, z, core = lax.axis_index("xh"), lax.axis_index("z"), lax.axis_index("c")
    me = xh * CORE + core
    sides = matching.reshape(tiles * 4, 4)
    grouped = matching.reshape(XH, Z, CORE, lines, 4)
    column = lax.dynamic_index_in_dim(grouped, z, 1, keepdims=False).reshape(XH * CORE * lines, 4)
    tile, side = column[:, 0], column[:, 1]
    beside = jnp.where(side < 2, 2, 0)[:, None] + jnp.arange(2)[None, :]
    corners = sides[tile[:, None] * 4 + beside]
    finish = (side[:, None] % 2) ^ corners[..., 2]

    row = lax.axis_index(ROW_AXES)
    cells = UNITS * strip
    piece = cells * lines
    width = ROWS * strip

    def place(tile, side):
        group = tile // here
        held = column_of(group) == me
        return held, ((group // CORE) % Z) * piece + (tile % here) * 4 + side

    def own(table):
        return lax.dynamic_slice_in_dim(table, me * lines, lines, 0)

    held, at = place(tile, side)
    columns = XH * CORE
    cell = np.arange(cells, dtype=np.int32)[None, :, None] * lines
    pick = jnp.where(held.reshape(columns, 1, lines), at.reshape(columns, 1, lines) + cell, -1)
    held, at = place(corners[..., 0], corners[..., 1])
    at = jnp.where(held, at, -Z * piece).reshape(columns, lines, 2).swapaxes(1, 2)
    depth = np.array([0, 1, 0, 1], np.int32)
    depth = jnp.where(row == 0, depth, strip - 1 - depth)[None, :, None] * lines
    pick = jnp.concatenate([pick, jnp.repeat(at, 2, axis=1) + depth], axis=1).reshape(-1)

    mine, my_corners = own(column), own(corners)
    sent = piece + 4 * lines
    source = column_of(mine[:, 0] // here)[None, :]
    source_corner = column_of(my_corners[..., 0] // here).T
    select = jnp.concatenate(
        [jnp.broadcast_to(source, (cells, lines)), jnp.repeat(source_corner, 2, axis=0)], axis=0
    ).reshape(-1) * sent + np.arange(sent, dtype=np.int32)

    flipped = jnp.broadcast_to(mine[:, 2:3] == 1, (lines, width)).reshape(-1)
    position = np.arange(width, dtype=np.int32)[None, :]
    line = np.arange(lines, dtype=np.int32)[:, None]
    count = lines * width

    def places(position, step, base):
        return (position * step + line * base).reshape(-1)

    kind = jnp.broadcast_to(mine[:, 1:2], (lines, width)).reshape(-1)
    kind = (kind[None, :, None] == np.arange(4, dtype=np.int32)[:, None, None]).astype(bf16)
    kind = jnp.broadcast_to(kind, (4, count, channels))
    ends = jnp.repeat(own(finish).T, 2, axis=0)
    turned = jnp.where(
        flipped, places(width - 1 - position, lines, 1), places(position, lines, 1)
    )
    flip = jnp.where(flipped, places(width - 1 - position, 1, width), places(position, 1, width))
    return {
        "pick": rows_of(pick, Z * piece),
        "select": rows_of(select, columns * sent),
        "lines": rows_of(places(position, lines, 1), count),
        "turned": rows_of(turned, count),
        "flip": rows_of(flip, count),
        "flipped": flipped,
        "side": mine[:, 1],
        "kind": kind,
        "corner": rows_of(ends.reshape(-1) * (4 * lines) + np.arange(4 * lines, dtype=np.int32), 8 * lines),
        "quarter": mine[:, 3],
        "quarter_corner": my_corners[..., 3].T,
        "row": row,
    }


def rows_of(index, count):
    return (index[:, None] == jnp.arange(count)[None, :]).astype(bf16)


def take_rows(choice, rows):
    return jnp.dot(choice, rows, preferred_element_type=f32).astype(bf16)


def turn_channels(lines, quarter):
    half = lines.shape[-1] // 2
    first, second = lines[..., :half], lines[..., half:]
    quarter = quarter.reshape(quarter.shape + (1,) * (lines.ndim - quarter.ndim))
    odd = quarter % 2 == 1
    lead = jnp.where(odd, second, first)
    trail = jnp.where(odd, first, second)
    lead = jnp.where((quarter == 1) | (quarter == 2), -lead, lead)
    trail = jnp.where((quarter == 2) | (quarter == 3), -trail, trail)
    return jnp.concatenate([lead, trail], axis=-1)


def to_here(lines, plan, order="flip"):
    sides = plan["quarter"].shape[0]
    rows = take_rows(plan[order], lines.reshape(-1, lines.shape[-1]))
    return turn_channels(rows.reshape(sides, -1, lines.shape[-1]), plan["quarter"])


def to_neighbour(lines, plan, order="flip"):
    sides = plan["quarter"].shape[0]
    rows = take_rows(plan[order], lines.reshape(-1, lines.shape[-1]))
    return turn_channels(rows.reshape(sides, -1, lines.shape[-1]), (4 - plan["quarter"]) % 4)


def outer_lines(field, margin, row):
    tiles, rows, columns, channels = field.shape
    strip = rows - 2 * margin
    width = ROWS * strip
    unit = np.arange(UNITS)[:, None, None]
    cell = np.arange(strip)[None, :, None]
    tile = np.arange(tiles)[None, None, :] * (rows * columns)
    target = np.arange(ROWS)[:, None, None, None]
    last = width + 2 * margin - 1
    sides = np.stack([unit + tile, last - unit + tile], axis=-1) + (margin + cell)[..., None] * columns

    def index_of(line):
        ends = tile + line * columns + margin + target * strip + cell
        return np.concatenate([ends.reshape(-1), sides.reshape(-1)]).astype(np.int32)

    index = jnp.where(row == ROWS - 1, index_of(rows - 1 - unit), index_of(unit))
    chosen = take_rows(rows_of(index, tiles * rows * columns), field.reshape(-1, channels))
    cut = ROWS * UNITS * strip * tiles
    return chosen[:cut].reshape(ROWS, -1, channels), chosen[cut:]


def own_borders(field, plan):
    tiles, rows, columns, channels = field.shape
    strip = rows - 2
    width = ROWS * strip
    row = plan["row"]
    side = np.arange(4)[None, :, None]
    tile = np.arange(tiles)[:, None, None] * (rows * columns)

    def places(at):
        end = np.where(side == 0, 1 + at, (rows - 1) * columns + 1 + at)
        along = (1 + at) * columns + np.where(side == 2, 0, width + 1)
        index = tile + np.where(side < 2, end, along)
        owner = np.where(side < 2, side * (ROWS - 1), at // strip) + 0 * tile
        return index.reshape(-1).astype(np.int32), owner.reshape(-1).astype(np.int32)

    at = np.arange(width)[None, None, :]
    straight, owner = places(at)
    turned, owner_turned = places(width - 1 - at)
    index = jnp.where(plan["flipped"], turned, straight)
    off = np.where(side < 2, 0, strip * columns) + 0 * tile + 0 * at
    index = index - row * off.reshape(-1).astype(np.int32)
    index = jnp.where(jnp.where(plan["flipped"], owner_turned, owner) == row, index, -1)
    chosen = take_rows(rows_of(index, tiles * rows * columns), field.reshape(-1, channels))
    return turn_channels(chosen.reshape(tiles * 4, width, channels), (4 - plan["quarter"]) % 4)


def share_ends(ends):
    return lax.all_to_all(ends, ROW_AXES, 0, 0, tiled=True)


def offer(ends, sides, tiles):
    channels = sides.shape[-1]
    half = sides.shape[0] // 2
    piece = 4 * half
    held = jnp.concatenate([ends[0], ends[ROWS - 1], sides], axis=0)
    order = np.arange(half, dtype=np.int32)[:, None]
    order = np.concatenate(
        [order, half + order, 2 * half + 2 * order, 2 * half + 2 * order + 1], axis=1
    ).reshape(-1)
    everywhere = np.tile(order, Z)
    spread = take_rows(rows_of(everywhere, piece), held).reshape(Z, piece, channels)
    return spread, take_rows(rows_of(order[: piece // UNITS], piece), held)


def exchange(spread, first_own, tiles, plan, rider=None):
    lines = tiles * 4
    line, channels = first_own.shape
    piece = UNITS * line
    width = ROWS * line // lines
    gathered = lax.all_to_all(spread, "z", 0, 0, tiled=True).reshape(Z * piece, channels)
    sent = take_rows(plan["pick"], gathered).reshape(XH * CORE, -1, channels)
    arrived = lax.all_to_all(sent, COLUMN_AXES, 0, 0, tiled=True).reshape(-1, channels)
    mine = jnp.concatenate([take_rows(plan["select"], arrived), first_own], axis=0)
    count = mine.shape[0]
    mine = jnp.broadcast_to(mine[None], (ROWS,) + mine.shape)
    if rider is not None:
        mine = jnp.concatenate([mine, rider], axis=1)
    whole = lax.all_to_all(mine, ROW_AXES, 0, 0, tiled=True)
    first = whole[:, :line].reshape(ROWS * line, channels)
    second = whole[:, line : 2 * line].reshape(ROWS * line, channels)
    own = whole[:, piece + 4 * lines : count].reshape(ROWS * line, channels)
    corner = whole[:: ROWS - 1, piece : piece + 4 * lines].reshape(8 * lines, channels)
    corner = take_rows(plan["corner"], corner).reshape(2, 2, lines, channels)
    corner = turn_channels(corner, plan["quarter_corner"][:, None])
    return (
        to_here(first, plan, "turned"),
        take_rows(plan["lines"], first).reshape(lines, width, channels),
        take_rows(plan["lines"], second).reshape(lines, width, channels),
        to_neighbour(own, plan, "turned"),
        corner,
        whole[:, count:],
    )


def by_side(cells, plan):
    blocks = [
        jnp.where((plan["side"] == side)[:, None, None], cells, jnp.zeros((), cells.dtype))
        for side in range(4)
    ]
    return jnp.concatenate(blocks, axis=-1)


def edge_terms(patch_ref, kind_ref, weight_ref, out_ref, cells_ref):
    depths, lines = patch_ref.shape[:2]
    width = patch_ref.shape[2] - 2
    for depth in range(depths):
        for line in range(lines):
            cells = patch_ref[depth, line]
            for tap in range(3):
                cells_ref[depth * 3 + tap, line * width : (line + 1) * width] = shifted(cells, tap)
    part = lines * width // 2
    for half in range(2):
        total = None
        for depth in range(depths):
            for tap in range(3):
                cells = cells_ref[depth * 3 + tap, half * part : (half + 1) * part]
                places = ((depth, tap), (2 - depth, tap), (tap, depth), (tap, 2 - depth))
                for side, (a, b) in enumerate(places):
                    term = jnp.dot(
                        cells * kind_ref[side, half * part : (half + 1) * part],
                        weight_ref[a, b],
                        preferred_element_type=f32,
                    )
                    total = term if total is None else total + term
        out_ref[half * part : (half + 1) * part] = total


def neighbour_edge(edge, inner, own, corner, kernel_weight, plan):
    lines, width, channels = own.shape
    patch = jnp.stack(
        [
            jnp.pad(own, ((0, 0), (1, 1), (0, 0))),
            jnp.concatenate([corner[0, 0][:, None], edge, corner[1, 0][:, None]], axis=1),
            jnp.concatenate([corner[0, 1][:, None], inner, corner[1, 1][:, None]], axis=1),
        ]
    )
    total = pl.pallas_call(
        edge_terms,
        out_shape=jax.ShapeDtypeStruct((lines * width, channels), f32),
        in_specs=[WHOLE] * 3,
        out_specs=WHOLE,
        scratch_shapes=[pltpu.VMEM((9, lines * width, channels), bf16)],
        compiler_params=ROOM,
        cost_estimate=CHEAP,
    )(patch, plan["kind"], kernel_weight)
    return total.reshape(lines, width, channels), patch


def neighbour_border(grads, kernel_weight, plan):
    width = grads.shape[1]
    w = kernel_weight
    spread = by_side(jnp.pad(grads, ((0, 0), (1, 1), (0, 0))), plan)
    total = None
    for tap in range(3):
        weights = jnp.concatenate(
            [w[0, 2 - tap], w[2, 2 - tap], w[2 - tap, 0], w[2 - tap, 2]], axis=1
        )
        term = lax.dot_general(
            spread[:, tap : tap + width],
            weights,
            (((2,), (1,)), ((), ())),
            preferred_element_type=f32,
        )
        total = term if total is None else total + term
    return total


def own_part(lines, margin, plan):
    strip = lines.shape[1] // ROWS
    padded = jnp.pad(lines, ((0, 0), (margin, margin), (0, 0)))
    return lax.dynamic_slice_in_dim(padded, plan["row"] * strip, strip + 2 * margin, 1)


def with_ghosts(strips, ghosts, margin, plan):
    row = plan["row"]
    above = jnp.where(row == 0, ghosts[:, 0], strips[:, margin - 1])
    below = jnp.where(row == ROWS - 1, ghosts[:, 1], strips[:, -margin])
    middle = jnp.concatenate(
        [strips[:, : margin - 1], above[:, None], strips[:, margin:-margin], below[:, None]]
        + ([strips[:, -margin + 1 :]] if margin > 1 else []),
        axis=1,
    )
    left = own_part(ghosts[:, 2], margin, plan)
    right = own_part(ghosts[:, 3], margin, plan)
    return jnp.concatenate([left[:, :, None], middle, right[:, :, None]], axis=2)


def add_borders(interior, routed, margin, plan):
    row = plan["row"]
    routed = routed.astype(f32)
    rows = interior.shape[1]
    index = jnp.arange(rows)[None, :, None, None]
    top = jnp.where((row == 0) & (index == margin), routed[:, 0][:, None], 0.0)
    bottom = jnp.where(
        (row == ROWS - 1) & (index == rows - 1 - margin), routed[:, 1][:, None], 0.0
    )
    column = jnp.arange(interior.shape[2])[None, None, :, None]
    left = own_part(routed[:, 2], margin, plan)[:, :, None]
    right = own_part(routed[:, 3], margin, plan)[:, :, None]
    sides = jnp.where(column == 0, left, 0.0) + jnp.where(
        column == interior.shape[2] - 1, right, 0.0
    )
    return interior + top + bottom + sides


def inside(rows, margin, width, plan):
    strip = width // ROWS
    place = plan["row"] * strip - margin + jnp.arange(rows)
    return ((place >= 0) & (place < width))[None, :, None, None]


def shifted(field, tap):
    return field.astype(f32)[tap : tap + field.shape[0] - 2].astype(field.dtype)


def convolve_cells(back, padded_ref, weight_ref, out_ref, cells_ref):
    tiles, rows, columns = out_ref.shape[:3]
    step = tiles * columns
    for row in range(rows + 2):
        for tile in range(tiles):
            at = row * step + tile * columns
            line = padded_ref[tile, row]
            for tap in range(3):
                cells_ref[tap, at : at + columns] = shifted(line, tap)
    for row in range(0, rows, 2):
        total = None
        for a in range(3):
            for b in range(3):
                cells = cells_ref[b, (row + a) * step : (row + a + 2) * step]
                weight = weight_ref[2 - a, 2 - b] if back else weight_ref[a, b]
                term = lax.dot_general(
                    cells,
                    weight,
                    (((1,), (1 if back else 0,)), ((), ())),
                    preferred_element_type=f32,
                )
                total = term if total is None else total + term
        for half in range(2):
            for tile in range(tiles):
                at = half * step + tile * columns
                out_ref[tile, row + half] = total[at : at + columns]


WHOLE = pl.BlockSpec(memory_space=pltpu.VMEM)
ROOM = pltpu.CompilerParams(vmem_limit_bytes=40 * 2**20)
CHEAP = pl.CostEstimate(flops=1000, bytes_accessed=1000, transcendentals=0)


def convolve(padded, kernel_weight, back=False):
    tiles, rows, columns, channels = padded.shape
    return pl.pallas_call(
        functools.partial(convolve_cells, back),
        out_shape=jax.ShapeDtypeStruct((tiles, rows - 2, columns - 2, channels), f32),
        in_specs=[WHOLE] * 2,
        out_specs=WHOLE,
        scratch_shapes=[pltpu.VMEM((3, tiles * rows * (columns - 2), channels), bf16)],
        compiler_params=ROOM,
        cost_estimate=CHEAP,
    )(padded, kernel_weight)


def with_columns(grads, before, after):
    return jnp.pad(grads, ((0, 0), (0, 0), (before, after), (0, 0)))


def strip_terms(padded_ref, grads_ref, out_ref, cells_ref, rows_ref):
    tiles, rows, columns = grads_ref.shape[:3]
    for row in range(rows + 2):
        for tile in range(tiles):
            at = (row * tiles + tile) * columns
            line = padded_ref[tile, row]
            for tap in range(3):
                cells_ref[tap, at : at + columns] = shifted(line, tap)
            if row < rows:
                rows_ref[at : at + columns] = grads_ref[tile, row]
    grads = rows_ref[...]
    step = tiles * columns
    for a in range(3):
        for b in range(3):
            out_ref[a * 3 + b] = lax.dot_general(
                cells_ref[b, a * step : (a + rows) * step],
                grads,
                (((0,), (0,)), ((), ())),
                preferred_element_type=f32,
            )


def border_terms(patch_ref, grads_ref, edges_ref, out_ref):
    depths, lines = patch_ref.shape[:2]
    width, channels = patch_ref.shape[2] - 2, patch_ref.shape[3]
    for depth in range(depths):
        for line in range(lines):
            cells = patch_ref[depth, line]
            for tap in range(3):
                edges_ref[tap, line * width : (line + 1) * width] = shifted(cells, tap)
        for tap in range(3):
            term = lax.dot_general(
                edges_ref[tap],
                grads_ref[...],
                (((0,), (0,)), ((), ())),
                preferred_element_type=f32,
            )
            places = ((depth, tap), (2 - depth, tap), (tap, depth), (tap, 2 - depth))
            for side, (a, b) in enumerate(places):
                out_ref[a * 3 + b] += term[:, side * channels : (side + 1) * channels]


def weight_grad(padded, grads, patch=None, edge_grads=None):
    tiles, rows, columns, channels = grads.shape
    scratch = [
        pltpu.VMEM((3, tiles * (rows + 2) * columns, channels), bf16),
        pltpu.VMEM((tiles * rows * columns, channels), bf16),
    ]
    operands = [padded, grads]
    if patch is None:
        kernel = strip_terms
    else:
        operands += [patch, edge_grads]
        scratch.append(pltpu.VMEM((3, edge_grads.shape[0], channels), bf16))

        def kernel(padded_ref, grads_ref, patch_ref, edge_ref, out_ref, cells, rows, edges):
            strip_terms(padded_ref, grads_ref, out_ref, cells, rows)
            border_terms(patch_ref, edge_ref, edges, out_ref)

    return pl.pallas_call(
        kernel,
        out_shape=jax.ShapeDtypeStruct((9, channels, channels), f32),
        in_specs=[WHOLE] * len(operands),
        out_specs=WHOLE,
        scratch_shapes=scratch,
        compiler_params=ROOM,
        cost_estimate=CHEAP,
    )(*operands)


def grouped_cells(field):
    tiles, rows, columns, channels = field.shape
    return field.reshape(tiles, rows // 2, 2, columns // 2, 2, channels)


def strided_shrink(field, kernel_weight):
    grouped = grouped_cells(field)
    total = None
    for row_tap in range(2):
        for col_tap in range(2):
            term = jnp.dot(
                grouped[:, :, row_tap, :, col_tap],
                kernel_weight[row_tap, col_tap],
                preferred_element_type=f32,
            )
            total = term if total is None else total + term
    return total


def upsample_back(grads, kernel_weight):
    tiles, rows, columns, channels = grads.shape
    stacked = []
    for row_tap in range(2):
        pieces = [
            lax.dot_general(
                grads,
                kernel_weight[row_tap, col_tap],
                (((3,), (1,)), ((), ())),
                preferred_element_type=f32,
            )
            for col_tap in range(2)
        ]
        stacked.append(jnp.stack(pieces, axis=3))
    return jnp.stack(stacked, axis=2).reshape(tiles, rows * 2, columns * 2, kernel_weight.shape[2])


def down_terms(cells_ref, grads_ref, out_ref):
    for tap in range(cells_ref.shape[0]):
        out_ref[tap] = lax.dot_general(
            cells_ref[tap],
            grads_ref[...],
            (((0,), (0,)), ((), ())),
            preferred_element_type=f32,
        )


def down_grad(field, grads):
    channels = field.shape[-1]
    cells = grouped_cells(field).transpose(2, 4, 0, 1, 3, 5).reshape(4, -1, channels)
    return pl.pallas_call(
        down_terms,
        out_shape=jax.ShapeDtypeStruct((4, channels, channels), f32),
        in_specs=[WHOLE] * 2,
        out_specs=WHOLE,
        compiler_params=ROOM,
        cost_estimate=CHEAP,
    )(cells, grads.reshape(-1, channels))


def silu(value):
    return value * jax.nn.sigmoid(value)


def silu_slope(value):
    sigma = jax.nn.sigmoid(value)
    return sigma * (1.0 + value * (1.0 - sigma))


SWAP = [(0, 1), (1, 0)]


def sum_pair(blocks):
    channels = blocks[0].shape[-1]
    core = lax.axis_index("c")
    rows = jnp.concatenate([block.reshape(-1, channels) for block in blocks], axis=0)
    first, second = rows[: rows.shape[0] // 2], rows[rows.shape[0] // 2 :]
    sent = jnp.where(core == 0, second, first).astype(bf16)
    held = jnp.where(core == 0, first, second) + lax.ppermute(sent, "c", SWAP).astype(f32)
    return held.astype(bf16).reshape(ROWS, -1, channels)


def sum_shards(held, factor):
    channels = held.shape[-1]
    held = held.astype(f32).sum(0)
    held = held.astype(bf16).reshape(XH * Z, -1, channels)
    held = lax.all_to_all(held, ("xh", "z"), 0, 0, tiled=True).astype(f32).sum(0)
    held = (held * factor).astype(bf16)
    return broadcast_all(held, ("xh", "z"), XH * Z).reshape(-1, channels)


def gather_sums(held, beside):
    channels = held.shape[-1]
    core = lax.axis_index("c")
    held = broadcast_all(held, ROW_AXES, ROWS).reshape(-1, channels)
    held, beside = lax.optimization_barrier((held, beside))
    other = lax.ppermute(held, "c", SWAP)
    first = jnp.where(core == 0, held, other)
    second = jnp.where(core == 0, other, held)
    both = jnp.concatenate([first, second], axis=0).astype(f32)
    return both.reshape(-1, channels, channels), beside


def body(activations, matching, first_kernel_weight, conv_second, reduce_kernel_weight, cotangent):
    tiles, strip, width, channels = activations.shape
    factor = 1.0 / math.sqrt(matching.shape[0] * width * width)

    first_rows = jnp.concatenate(
        [activations[:, :4].reshape(tiles, 4 * width, channels), cotangent[:, 0]], axis=1
    )
    last_rows = jnp.concatenate(
        [activations[:, -4:].reshape(tiles, 4 * width, channels), cotangent[:, -1]], axis=1
    )
    def sides_of(lines):
        return lines.reshape(tiles, 4, width, channels)

    ends, sides = outer_lines(activations, 0, lax.axis_index(ROW_AXES))
    pieces, first_own = offer(share_ends(ends), sides, tiles)
    pieces, first_rows, last_rows, matching = lax.optimization_barrier(
        (pieces, first_rows, last_rows, matching)
    )
    plan = routing(matching, strip, channels)
    ghosts, edge, inner, own, corner, _ = exchange(pieces, first_own, tiles, plan)
    above = lax.ppermute(last_rows, ROW_AXES, [(i, i + 1) for i in range(ROWS - 1)])
    below = lax.ppermute(first_rows, ROW_AXES, [(i + 1, i) for i in range(ROWS - 1)])
    cells = 4 * width
    wide_input = jnp.concatenate(
        [
            above[:, :cells].reshape(tiles, 4, width, channels),
            activations,
            below[:, :cells].reshape(tiles, 4, width, channels),
        ],
        axis=1,
    )
    wide_cotangent = jnp.concatenate(
        [above[:, None, cells:], cotangent, below[:, None, cells:]], axis=1
    )

    edge_first, edge_cells = neighbour_edge(edge, inner, own, corner, first_kernel_weight, plan)
    padded_input = with_ghosts(wide_input, sides_of(ghosts), 4, plan)
    pre_first = convolve(padded_input, first_kernel_weight)
    hidden_first = jnp.where(
        inside(strip + 6, 3, width, plan), silu(pre_first).astype(bf16), jnp.zeros((), bf16)
    )

    ghosts = sides_of(to_here(silu(edge_first).astype(bf16), plan))
    padded_hidden = with_ghosts(hidden_first, ghosts, 3, plan)
    pre_second = convolve(padded_hidden, conv_second)
    hidden_second = silu(pre_second[:, 2:-2]).astype(bf16)
    output = strided_shrink(hidden_second, reduce_kernel_weight).astype(bf16)
    grad_second = (
        upsample_back(wide_cotangent, reduce_kernel_weight) * silu_slope(pre_second)
    ).astype(bf16)

    spread = convolve(with_columns(grad_second, 2, 2 + EXTRA), conv_second, True)
    narrow = spread.astype(bf16)
    ends, sides = outer_lines(narrow, 1, plan["row"])
    pieces, first_own = offer(share_ends(ends), sides, tiles)
    pieces, held_spread, held_narrow = lax.optimization_barrier((pieces, spread, narrow))

    edge_slope = silu_slope(edge_first)
    slope_first = silu_slope(pre_first[:, 2:-2])
    own_grad = (held_spread[:, 1:-1, 1 : width + 1] * slope_first[:, 1:-1]).astype(bf16)
    border_grad = (own_borders(held_narrow, plan).astype(f32) * edge_slope).astype(bf16)
    edge_grad = by_side(border_grad, plan).reshape(tiles * 4 * width, 4 * channels)
    parts = sum_pair(
        [
            weight_grad(padded_input[:, 3:-3], own_grad, edge_cells, edge_grad),
            weight_grad(padded_hidden[:, 2:-2], grad_second[:, 2:-2]),
            down_grad(hidden_second, cotangent),
        ]
    )

    routed, _, inner, own, corner, parts = exchange(
        pieces, first_own, tiles, plan, parts
    )
    routed = sides_of(routed)
    grad_first_hidden = add_borders(spread[:, :, 1 : width + 1], routed, 1, plan)
    grad_first = jnp.where(
        inside(strip + 2, 1, width, plan),
        (grad_first_hidden * slope_first).astype(bf16),
        jnp.zeros((), bf16),
    )

    place = jnp.arange(width)[None, :, None]
    corner = corner.astype(f32)
    edge_hidden = (
        inner.astype(f32)
        + own.astype(f32)
        + jnp.where(place == 0, corner[0, 0][:, None], 0.0)
        + jnp.where(place == width - 1, corner[1, 0][:, None], 0.0)
    )
    edge_grad = (edge_hidden * edge_slope).astype(bf16)
    routed = sides_of(to_here(neighbour_border(edge_grad, first_kernel_weight, plan).astype(bf16), plan))
    spread = convolve(with_columns(grad_first, 1, 1), first_kernel_weight, True)
    shards, spread = lax.optimization_barrier((sum_shards(parts, factor), spread))
    grad_activations = add_borders(spread, routed, 0, plan).astype(bf16)
    summed, (output, grad_activations) = gather_sums(shards, (output, grad_activations))
    square = (channels, channels)
    return (
        output,
        grad_activations,
        summed[:9].reshape((3, 3) + square),
        summed[9:18].reshape((3, 3) + square),
        summed[18:].reshape((2, 2) + square),
    )


def solution(mesh):
    fine = Mesh(mesh.devices.reshape(XH, Z, CORE, Y, XL), TILE_AXES + ROW_AXES)
    placed = P(TILE_AXES, ROW_AXES, None, None)
    return jax.shard_map(
        body,
        mesh=fine,
        in_specs=(placed, P(), P(), P(), P(), placed),
        out_specs=(placed, placed, P(), P(), P()),
        check_vma=False,
    )
```

```python
import functools
import math

import jax
import jax.numpy as jnp
import numpy as np
from jax import lax
from jax.experimental import pallas as pl
from jax.experimental.pallas import tpu as pltpu
from jax.sharding import Mesh, PartitionSpec as P

XH, Z, CORE, Y, XL = 2, 8, 2, 4, 2
ROWS = Y * XL
UNITS = 2
EXTRA = 14
TILE_AXES = ("xh", "z", "c")
ROW_AXES = ("y", "xl")
COLUMN_AXES = ("xh", "c")
f32 = jnp.float32
bf16 = jnp.bfloat16


def broadcast_all(piece, axes, count):
    return lax.all_to_all(
        jnp.broadcast_to(piece[None], (count,) + piece.shape), axes, 0, 0, tiled=True
    )


def column_of(group):
    return (group // (Z * CORE)) * CORE + group % CORE


def routing(matching, strip):
    tiles = matching.shape[0]
    here = tiles // (XH * Z * CORE)
    lines = here * 4
    xh, z, core = lax.axis_index("xh"), lax.axis_index("z"), lax.axis_index("c")
    me = xh * CORE + core
    sides = matching.reshape(tiles * 4, 4)
    grouped = matching.reshape(XH, Z, CORE, lines, 4)
    column = lax.dynamic_index_in_dim(grouped, z, 1, keepdims=False).reshape(XH * CORE * lines, 4)
    tile, side = column[:, 0], column[:, 1]
    beside = jnp.where(side < 2, 2, 0)[:, None] + jnp.arange(2)[None, :]
    corners = sides[tile[:, None] * 4 + beside]
    finish = (side[:, None] % 2) ^ corners[..., 2]

    row = lax.axis_index(ROW_AXES)
    cells = UNITS * strip
    piece = cells * lines
    width = ROWS * strip

    def place(tile, side):
        group = tile // here
        held = column_of(group) == me
        return held, ((group // CORE) % Z) * piece + (tile % here) * 4 + side

    def own(table):
        return lax.dynamic_slice_in_dim(table, me * lines, lines, 0)

    held, at = place(tile, side)
    columns = XH * CORE
    cell = np.arange(cells, dtype=np.int32)[None, :, None] * lines
    pick = jnp.where(held.reshape(columns, 1, lines), at.reshape(columns, 1, lines) + cell, -1)
    held, at = place(corners[..., 0], corners[..., 1])
    at = jnp.where(held, at, -Z * piece).reshape(columns, lines, 2).swapaxes(1, 2)
    depth = np.array([0, 1, 0, 1], np.int32)
    depth = jnp.where(row == 0, depth, strip - 1 - depth)[None, :, None] * lines
    pick = jnp.concatenate([pick, jnp.repeat(at, 2, axis=1) + depth], axis=1).reshape(-1)

    mine, my_corners = own(column), own(corners)
    sent = piece + 4 * lines
    source = column_of(mine[:, 0] // here)[None, :]
    source_corner = column_of(my_corners[..., 0] // here).T
    select = jnp.concatenate(
        [jnp.broadcast_to(source, (cells, lines)), jnp.repeat(source_corner, 2, axis=0)], axis=0
    ).reshape(-1) * sent + np.arange(sent, dtype=np.int32)

    flipped = jnp.broadcast_to(mine[:, 2:3] == 1, (lines, width)).reshape(-1)
    position = np.arange(width, dtype=np.int32)[None, :]
    line = np.arange(lines, dtype=np.int32)[:, None]
    count = lines * width

    def places(position, step, base):
        return (position * step + line * base).reshape(-1)

    turned = jnp.where(
        flipped, places(width - 1 - position, lines, 1), places(position, lines, 1)
    )
    flip = jnp.where(flipped, places(width - 1 - position, 1, width), places(position, 1, width))
    return {
        "pick": rows_of(pick, Z * piece),
        "select": rows_of(select, columns * sent),
        "lines": rows_of(places(position, lines, 1), count),
        "turned": rows_of(turned, count),
        "flip": rows_of(flip, count),
        "flipped": flipped,
        "side": mine[:, 1],
        "quarter": mine[:, 3],
        "quarter_corner": my_corners[..., 3].T,
        "finish": own(finish).T == 1,
        "row": row,
    }


def rows_of(index, count):
    return (index[:, None] == jnp.arange(count)[None, :]).astype(bf16)


def take_rows(choice, rows):
    return jnp.dot(choice, rows, preferred_element_type=f32).astype(bf16)


def turn_channels(lines, quarter):
    half = lines.shape[-1] // 2
    first, second = lines[..., :half], lines[..., half:]
    quarter = quarter.reshape(quarter.shape + (1,) * (lines.ndim - quarter.ndim))
    odd = quarter % 2 == 1
    lead = jnp.where(odd, second, first)
    trail = jnp.where(odd, first, second)
    lead = jnp.where((quarter == 1) | (quarter == 2), -lead, lead)
    trail = jnp.where((quarter == 2) | (quarter == 3), -trail, trail)
    return jnp.concatenate([lead, trail], axis=-1)


def to_here(lines, plan, order="flip"):
    sides = plan["quarter"].shape[0]
    rows = take_rows(plan[order], lines.reshape(-1, lines.shape[-1]))
    return turn_channels(rows.reshape(sides, -1, lines.shape[-1]), plan["quarter"])


def to_neighbour(lines, plan, order="flip"):
    sides = plan["quarter"].shape[0]
    rows = take_rows(plan[order], lines.reshape(-1, lines.shape[-1]))
    return turn_channels(rows.reshape(sides, -1, lines.shape[-1]), (4 - plan["quarter"]) % 4)


def outer_lines(field, margin, row):
    tiles, rows, columns, channels = field.shape
    strip = rows - 2 * margin
    width = ROWS * strip
    unit = np.arange(UNITS)[:, None, None]
    cell = np.arange(strip)[None, :, None]
    tile = np.arange(tiles)[None, None, :] * (rows * columns)
    target = np.arange(ROWS)[:, None, None, None]
    last = width + 2 * margin - 1
    sides = np.stack([unit + tile, last - unit + tile], axis=-1) + (margin + cell)[..., None] * columns

    def index_of(line):
        ends = tile + line * columns + margin + target * strip + cell
        return np.concatenate([ends.reshape(-1), sides.reshape(-1)]).astype(np.int32)

    index = jnp.where(row == ROWS - 1, index_of(rows - 1 - unit), index_of(unit))
    chosen = take_rows(rows_of(index, tiles * rows * columns), field.reshape(-1, channels))
    cut = ROWS * UNITS * strip * tiles
    return chosen[:cut].reshape(ROWS, -1, channels), chosen[cut:]


def own_borders(field, plan):
    tiles, rows, columns, channels = field.shape
    strip = rows - 2
    width = ROWS * strip
    row = plan["row"]
    side = np.arange(4)[None, :, None]
    tile = np.arange(tiles)[:, None, None] * (rows * columns)

    def places(at):
        end = np.where(side == 0, 1 + at, (rows - 1) * columns + 1 + at)
        along = (1 + at) * columns + np.where(side == 2, 0, width + 1)
        index = tile + np.where(side < 2, end, along)
        owner = np.where(side < 2, side * (ROWS - 1), at // strip) + 0 * tile
        return index.reshape(-1).astype(np.int32), owner.reshape(-1).astype(np.int32)

    at = np.arange(width)[None, None, :]
    straight, owner = places(at)
    turned, owner_turned = places(width - 1 - at)
    index = jnp.where(plan["flipped"], turned, straight)
    off = np.where(side < 2, 0, strip * columns) + 0 * tile + 0 * at
    index = index - row * off.reshape(-1).astype(np.int32)
    index = jnp.where(jnp.where(plan["flipped"], owner_turned, owner) == row, index, -1)
    chosen = take_rows(rows_of(index, tiles * rows * columns), field.reshape(-1, channels))
    return turn_channels(chosen.reshape(tiles * 4, width, channels), (4 - plan["quarter"]) % 4)


def share_ends(ends):
    return lax.all_to_all(ends, ROW_AXES, 0, 0, tiled=True)


def offer(ends, sides, tiles):
    channels = sides.shape[-1]
    half = sides.shape[0] // 2
    piece = 4 * half
    held = jnp.concatenate([ends[0], ends[ROWS - 1], sides], axis=0)
    order = np.arange(half, dtype=np.int32)[:, None]
    order = np.concatenate(
        [order, half + order, 2 * half + 2 * order, 2 * half + 2 * order + 1], axis=1
    ).reshape(-1)
    everywhere = np.tile(order, Z)
    spread = take_rows(rows_of(everywhere, piece), held).reshape(Z, piece, channels)
    return spread, take_rows(rows_of(order[: piece // UNITS], piece), held)


def exchange(spread, first_own, tiles, plan, rider=None, later=()):
    lines = tiles * 4
    line, channels = first_own.shape
    piece = UNITS * line
    width = ROWS * line // lines
    gathered = lax.all_to_all(spread, "z", 0, 0, tiled=True).reshape(Z * piece, channels)
    gathered, later = lax.optimization_barrier((gathered, later))
    sent = take_rows(plan["pick"], gathered).reshape(XH * CORE, -1, channels)
    arrived = lax.all_to_all(sent, COLUMN_AXES, 0, 0, tiled=True).reshape(-1, channels)
    mine = jnp.concatenate([take_rows(plan["select"], arrived), first_own], axis=0)
    count = mine.shape[0]
    mine = jnp.broadcast_to(mine[None], (ROWS,) + mine.shape)
    if rider is not None:
        mine = jnp.concatenate([mine, rider], axis=1)
    whole = lax.all_to_all(mine, ROW_AXES, 0, 0, tiled=True)
    first = whole[:, :line].reshape(ROWS * line, channels)
    second = whole[:, line : 2 * line].reshape(ROWS * line, channels)
    own = whole[:, piece + 4 * lines : count].reshape(ROWS * line, channels)
    corner = whole[:, piece : piece + 4 * lines].reshape(ROWS, 2, 2, lines, channels)
    corner = jnp.where(plan["finish"][:, None, :, None], corner[ROWS - 1], corner[0])
    corner = turn_channels(corner, plan["quarter_corner"][:, None])
    return (
        to_here(first, plan, "turned"),
        take_rows(plan["lines"], first).reshape(lines, width, channels),
        take_rows(plan["lines"], second).reshape(lines, width, channels),
        to_neighbour(own, plan, "turned"),
        corner,
        whole[:, count:],
        later,
    )


def by_side(cells, plan):
    blocks = [
        jnp.where((plan["side"] == side)[:, None, None], cells, jnp.zeros((), cells.dtype))
        for side in range(4)
    ]
    return jnp.concatenate(blocks, axis=-1)


def edge_terms(patch_ref, side_ref, weight_ref, out_ref, cells_ref, kind_ref):
    depths, lines = patch_ref.shape[:2]
    width = patch_ref.shape[2] - 2
    for depth in range(depths):
        for line in range(lines):
            cells = patch_ref[depth, line]
            for tap in range(3):
                cells_ref[depth * 3 + tap, line * width : (line + 1) * width] = shifted(cells, tap)
    for line in range(lines):
        for side in range(4):
            kind = jnp.full((width, kind_ref.shape[2]), side_ref[line] == side, f32)
            kind_ref[side, line * width : (line + 1) * width] = kind.astype(bf16)
    part = lines * width // 2
    for half in range(2):
        total = None
        for depth in range(depths):
            for tap in range(3):
                cells = cells_ref[depth * 3 + tap, half * part : (half + 1) * part]
                places = ((depth, tap), (2 - depth, tap), (tap, depth), (tap, 2 - depth))
                for side, (a, b) in enumerate(places):
                    term = jnp.dot(
                        cells * kind_ref[side, half * part : (half + 1) * part],
                        weight_ref[a, b],
                        preferred_element_type=f32,
                    )
                    total = term if total is None else total + term
        out_ref[half * part : (half + 1) * part] = total


def neighbour_edge(edge, inner, own, corner, kernel_weight, plan):
    lines, width, channels = own.shape
    patch = jnp.stack(
        [
            jnp.pad(own, ((0, 0), (1, 1), (0, 0))),
            jnp.concatenate([corner[0, 0][:, None], edge, corner[1, 0][:, None]], axis=1),
            jnp.concatenate([corner[0, 1][:, None], inner, corner[1, 1][:, None]], axis=1),
        ]
    )
    total = pl.pallas_call(
        edge_terms,
        out_shape=jax.ShapeDtypeStruct((lines * width, channels), f32),
        in_specs=[WHOLE, pl.BlockSpec(memory_space=pltpu.SMEM), WHOLE],
        out_specs=WHOLE,
        scratch_shapes=[
            pltpu.VMEM((9, lines * width, channels), bf16),
            pltpu.VMEM((4, lines * width, channels), bf16),
        ],
        compiler_params=ROOM,
        cost_estimate=CHEAP,
    )(patch, plan["side"], kernel_weight)
    return total.reshape(lines, width, channels), patch


def neighbour_border(grads, kernel_weight, plan):
    width = grads.shape[1]
    w = kernel_weight
    spread = by_side(jnp.pad(grads, ((0, 0), (1, 1), (0, 0))), plan)
    total = None
    for tap in range(3):
        weights = jnp.concatenate(
            [w[0, 2 - tap], w[2, 2 - tap], w[2 - tap, 0], w[2 - tap, 2]], axis=1
        )
        term = lax.dot_general(
            spread[:, tap : tap + width],
            weights,
            (((2,), (1,)), ((), ())),
            preferred_element_type=f32,
        )
        total = term if total is None else total + term
    return total


def own_part(lines, margin, plan):
    strip = lines.shape[1] // ROWS
    padded = jnp.pad(lines, ((0, 0), (margin, margin), (0, 0)))
    return lax.dynamic_slice_in_dim(padded, plan["row"] * strip, strip + 2 * margin, 1)


def with_ghosts(strips, ghosts, margin, plan):
    row = plan["row"]
    above = jnp.where(row == 0, ghosts[:, 0], strips[:, margin - 1])
    below = jnp.where(row == ROWS - 1, ghosts[:, 1], strips[:, -margin])
    middle = jnp.concatenate(
        [strips[:, : margin - 1], above[:, None], strips[:, margin:-margin], below[:, None]]
        + ([strips[:, -margin + 1 :]] if margin > 1 else []),
        axis=1,
    )
    left = own_part(ghosts[:, 2], margin, plan)
    right = own_part(ghosts[:, 3], margin, plan)
    return jnp.concatenate([left[:, :, None], middle, right[:, :, None]], axis=2)


def add_borders(interior, routed, margin, plan):
    row = plan["row"]
    routed = routed.astype(f32)
    rows = interior.shape[1]
    index = jnp.arange(rows)[None, :, None, None]
    top = jnp.where((row == 0) & (index == margin), routed[:, 0][:, None], 0.0)
    bottom = jnp.where(
        (row == ROWS - 1) & (index == rows - 1 - margin), routed[:, 1][:, None], 0.0
    )
    column = jnp.arange(interior.shape[2])[None, None, :, None]
    left = own_part(routed[:, 2], margin, plan)[:, :, None]
    right = own_part(routed[:, 3], margin, plan)[:, :, None]
    sides = jnp.where(column == 0, left, 0.0) + jnp.where(
        column == interior.shape[2] - 1, right, 0.0
    )
    return interior + top + bottom + sides


def inside(rows, margin, width, plan):
    strip = width // ROWS
    place = plan["row"] * strip - margin + jnp.arange(rows)
    return ((place >= 0) & (place < width))[None, :, None, None]


def shifted(field, tap):
    return field.astype(f32)[tap : tap + field.shape[0] - 2].astype(field.dtype)


def convolve_cells(back, padded_ref, weight_ref, out_ref, cells_ref):
    tiles, rows, columns = out_ref.shape[:3]
    step = tiles * columns
    for row in range(rows + 2):
        for tile in range(tiles):
            at = row * step + tile * columns
            line = padded_ref[tile, row]
            for tap in range(3):
                cells_ref[tap, at : at + columns] = shifted(line, tap)
    for row in range(0, rows, 2):
        total = None
        for a in range(3):
            for b in range(3):
                cells = cells_ref[b, (row + a) * step : (row + a + 2) * step]
                weight = weight_ref[2 - a, 2 - b] if back else weight_ref[a, b]
                term = lax.dot_general(
                    cells,
                    weight,
                    (((1,), (1 if back else 0,)), ((), ())),
                    preferred_element_type=f32,
                )
                total = term if total is None else total + term
        for half in range(2):
            for tile in range(tiles):
                at = half * step + tile * columns
                out_ref[tile, row + half] = total[at : at + columns]


WHOLE = pl.BlockSpec(memory_space=pltpu.VMEM)
ROOM = pltpu.CompilerParams(vmem_limit_bytes=40 * 2**20)
CHEAP = pl.CostEstimate(flops=1000, bytes_accessed=1000, transcendentals=0)


def convolve(padded, kernel_weight, back=False):
    tiles, rows, columns, channels = padded.shape
    return pl.pallas_call(
        functools.partial(convolve_cells, back),
        out_shape=jax.ShapeDtypeStruct((tiles, rows - 2, columns - 2, channels), f32),
        in_specs=[WHOLE] * 2,
        out_specs=WHOLE,
        scratch_shapes=[pltpu.VMEM((3, tiles * rows * (columns - 2), channels), bf16)],
        compiler_params=ROOM,
        cost_estimate=CHEAP,
    )(padded, kernel_weight)


def with_columns(grads, before, after):
    return jnp.pad(grads, ((0, 0), (0, 0), (before, after), (0, 0)))


def strip_terms(padded_ref, grads_ref, out_ref, cells_ref, rows_ref):
    tiles, rows, columns = grads_ref.shape[:3]
    for row in range(rows + 2):
        for tile in range(tiles):
            at = (row * tiles + tile) * columns
            line = padded_ref[tile, row]
            for tap in range(3):
                cells_ref[tap, at : at + columns] = shifted(line, tap)
            if row < rows:
                rows_ref[at : at + columns] = grads_ref[tile, row]
    grads = rows_ref[...]
    step = tiles * columns
    for a in range(3):
        for b in range(3):
            out_ref[a * 3 + b] = lax.dot_general(
                cells_ref[b, a * step : (a + rows) * step],
                grads,
                (((0,), (0,)), ((), ())),
                preferred_element_type=f32,
            )


def border_terms(patch_ref, grads_ref, edges_ref, out_ref):
    depths, lines = patch_ref.shape[:2]
    width, channels = patch_ref.shape[2] - 2, patch_ref.shape[3]
    for depth in range(depths):
        for line in range(lines):
            cells = patch_ref[depth, line]
            for tap in range(3):
                edges_ref[tap, line * width : (line + 1) * width] = shifted(cells, tap)
        for tap in range(3):
            term = lax.dot_general(
                edges_ref[tap],
                grads_ref[...],
                (((0,), (0,)), ((), ())),
                preferred_element_type=f32,
            )
            places = ((depth, tap), (2 - depth, tap), (tap, depth), (tap, 2 - depth))
            for side, (a, b) in enumerate(places):
                out_ref[a * 3 + b] += term[:, side * channels : (side + 1) * channels]


def weight_grad(padded, grads, patch=None, edge_grads=None):
    tiles, rows, columns, channels = grads.shape
    scratch = [
        pltpu.VMEM((3, tiles * (rows + 2) * columns, channels), bf16),
        pltpu.VMEM((tiles * rows * columns, channels), bf16),
    ]
    operands = [padded, grads]
    if patch is None:
        kernel = strip_terms
    else:
        operands += [patch, edge_grads]
        scratch.append(pltpu.VMEM((3, edge_grads.shape[0], channels), bf16))

        def kernel(padded_ref, grads_ref, patch_ref, edge_ref, out_ref, cells, rows, edges):
            strip_terms(padded_ref, grads_ref, out_ref, cells, rows)
            border_terms(patch_ref, edge_ref, edges, out_ref)

    return pl.pallas_call(
        kernel,
        out_shape=jax.ShapeDtypeStruct((9, channels, channels), f32),
        in_specs=[WHOLE] * len(operands),
        out_specs=WHOLE,
        scratch_shapes=scratch,
        compiler_params=ROOM,
        cost_estimate=CHEAP,
    )(*operands)


def grouped_cells(field):
    tiles, rows, columns, channels = field.shape
    return field.reshape(tiles, rows // 2, 2, columns // 2, 2, channels)


def strided_shrink(field, kernel_weight):
    grouped = grouped_cells(field)
    total = None
    for row_tap in range(2):
        for col_tap in range(2):
            term = jnp.dot(
                grouped[:, :, row_tap, :, col_tap],
                kernel_weight[row_tap, col_tap],
                preferred_element_type=f32,
            )
            total = term if total is None else total + term
    return total


def upsample_back(grads, kernel_weight):
    tiles, rows, columns, channels = grads.shape
    stacked = []
    for row_tap in range(2):
        pieces = [
            lax.dot_general(
                grads,
                kernel_weight[row_tap, col_tap],
                (((3,), (1,)), ((), ())),
                preferred_element_type=f32,
            )
            for col_tap in range(2)
        ]
        stacked.append(jnp.stack(pieces, axis=3))
    return jnp.stack(stacked, axis=2).reshape(tiles, rows * 2, columns * 2, kernel_weight.shape[2])


def down_terms(cells_ref, grads_ref, out_ref):
    for tap in range(cells_ref.shape[0]):
        out_ref[tap] = lax.dot_general(
            cells_ref[tap],
            grads_ref[...],
            (((0,), (0,)), ((), ())),
            preferred_element_type=f32,
        )


def down_grad(field, grads):
    channels = field.shape[-1]
    cells = grouped_cells(field).transpose(2, 4, 0, 1, 3, 5).reshape(4, -1, channels)
    return pl.pallas_call(
        down_terms,
        out_shape=jax.ShapeDtypeStruct((4, channels, channels), f32),
        in_specs=[WHOLE] * 2,
        out_specs=WHOLE,
        compiler_params=ROOM,
        cost_estimate=CHEAP,
    )(cells, grads.reshape(-1, channels))


def silu(value):
    return value * jax.nn.sigmoid(value)


def silu_slope(value):
    sigma = jax.nn.sigmoid(value)
    return sigma * (1.0 + value * (1.0 - sigma))


SWAP = [(0, 1), (1, 0)]


def sum_pair(blocks):
    channels = blocks[0].shape[-1]
    core = lax.axis_index("c")
    rows = jnp.concatenate([block.reshape(-1, channels) for block in blocks], axis=0)
    first, second = rows[: rows.shape[0] // 2], rows[rows.shape[0] // 2 :]
    sent = jnp.where(core == 0, second, first).astype(bf16)
    held = jnp.where(core == 0, first, second) + lax.ppermute(sent, "c", SWAP).astype(f32)
    return held.astype(bf16).reshape(ROWS, -1, channels)


def sum_shards(held, factor):
    channels = held.shape[-1]
    held = held.astype(f32).sum(0)
    held = held.astype(bf16).reshape(XH * Z, -1, channels)
    held = lax.all_to_all(held, ("xh", "z"), 0, 0, tiled=True).astype(f32).sum(0)
    held = (held * factor).astype(bf16)
    return broadcast_all(held, ("xh", "z"), XH * Z).reshape(-1, channels)


def gather_sums(held, beside):
    channels = held.shape[-1]
    core = lax.axis_index("c")
    held = broadcast_all(held, ROW_AXES, ROWS).reshape(-1, channels)
    held, beside = lax.optimization_barrier((held, beside))
    other = lax.ppermute(held, "c", SWAP)
    first = jnp.where(core == 0, held, other)
    second = jnp.where(core == 0, other, held)
    both = jnp.concatenate([first, second], axis=0).astype(f32)
    return both.reshape(-1, channels, channels), beside


def body(activations, matching, first_kernel_weight, conv_second, reduce_kernel_weight, cotangent):
    tiles, strip, width, channels = activations.shape
    factor = 1.0 / math.sqrt(matching.shape[0] * width * width)

    first_rows = jnp.concatenate(
        [activations[:, :4].reshape(tiles, 4 * width, channels), cotangent[:, 0]], axis=1
    )
    last_rows = jnp.concatenate(
        [activations[:, -4:].reshape(tiles, 4 * width, channels), cotangent[:, -1]], axis=1
    )
    def sides_of(lines):
        return lines.reshape(tiles, 4, width, channels)

    ends, sides = outer_lines(activations, 0, lax.axis_index(ROW_AXES))
    pieces, first_own = offer(share_ends(ends), sides, tiles)
    pieces, matching = lax.optimization_barrier((pieces, matching))
    plan = routing(matching, strip)
    ghosts, edge, inner, own, corner, _, (first_rows, last_rows) = exchange(
        pieces, first_own, tiles, plan, None, (first_rows, last_rows)
    )
    above = lax.ppermute(last_rows, ROW_AXES, [(i, i + 1) for i in range(ROWS - 1)])
    below = lax.ppermute(first_rows, ROW_AXES, [(i + 1, i) for i in range(ROWS - 1)])
    cells = 4 * width
    wide_input = jnp.concatenate(
        [
            above[:, :cells].reshape(tiles, 4, width, channels),
            activations,
            below[:, :cells].reshape(tiles, 4, width, channels),
        ],
        axis=1,
    )
    wide_cotangent = jnp.concatenate(
        [above[:, None, cells:], cotangent, below[:, None, cells:]], axis=1
    )

    edge_first, edge_cells = neighbour_edge(edge, inner, own, corner, first_kernel_weight, plan)
    padded_input = with_ghosts(wide_input, sides_of(ghosts), 4, plan)
    pre_first = convolve(padded_input, first_kernel_weight)
    hidden_first = jnp.where(
        inside(strip + 6, 3, width, plan), silu(pre_first).astype(bf16), jnp.zeros((), bf16)
    )

    ghosts = sides_of(to_here(silu(edge_first).astype(bf16), plan))
    padded_hidden = with_ghosts(hidden_first, ghosts, 3, plan)
    pre_second = convolve(padded_hidden, conv_second)
    hidden_second = silu(pre_second[:, 2:-2]).astype(bf16)
    output = strided_shrink(hidden_second, reduce_kernel_weight).astype(bf16)
    grad_second = (
        upsample_back(wide_cotangent, reduce_kernel_weight) * silu_slope(pre_second)
    ).astype(bf16)

    spread = convolve(with_columns(grad_second, 2, 2 + EXTRA), conv_second, True)
    narrow = spread.astype(bf16)
    ends, sides = outer_lines(narrow, 1, plan["row"])
    pieces, first_own = offer(share_ends(ends), sides, tiles)
    pieces, held_spread, held_narrow = lax.optimization_barrier((pieces, spread, narrow))

    edge_slope = silu_slope(edge_first)
    slope_first = silu_slope(pre_first[:, 2:-2])
    own_grad = (held_spread[:, 1:-1, 1 : width + 1] * slope_first[:, 1:-1]).astype(bf16)
    border_grad = (own_borders(held_narrow, plan).astype(f32) * edge_slope).astype(bf16)
    edge_grad = by_side(border_grad, plan).reshape(tiles * 4 * width, 4 * channels)
    parts = sum_pair(
        [
            weight_grad(padded_input[:, 3:-3], own_grad, edge_cells, edge_grad),
            weight_grad(padded_hidden[:, 2:-2], grad_second[:, 2:-2]),
            down_grad(hidden_second, cotangent),
        ]
    )

    routed, _, inner, own, corner, parts, _ = exchange(
        pieces, first_own, tiles, plan, parts
    )
    routed = sides_of(routed)
    grad_first_hidden = add_borders(spread[:, :, 1 : width + 1], routed, 1, plan)
    grad_first = jnp.where(
        inside(strip + 2, 1, width, plan),
        (grad_first_hidden * slope_first).astype(bf16),
        jnp.zeros((), bf16),
    )

    place = jnp.arange(width)[None, :, None]
    corner = corner.astype(f32)
    edge_hidden = (
        inner.astype(f32)
        + own.astype(f32)
        + jnp.where(place == 0, corner[0, 0][:, None], 0.0)
        + jnp.where(place == width - 1, corner[1, 0][:, None], 0.0)
    )
    edge_grad = (edge_hidden * edge_slope).astype(bf16)
    routed = sides_of(to_here(neighbour_border(edge_grad, first_kernel_weight, plan).astype(bf16), plan))
    spread = convolve(with_columns(grad_first, 1, 1), first_kernel_weight, True)
    shards, spread = lax.optimization_barrier((sum_shards(parts, factor), spread))
    grad_activations = add_borders(spread, routed, 0, plan).astype(bf16)
    summed, (output, grad_activations) = gather_sums(shards, (output, grad_activations))
    square = (channels, channels)
    return (
        output,
        grad_activations,
        summed[:9].reshape((3, 3) + square),
        summed[9:18].reshape((3, 3) + square),
        summed[18:].reshape((2, 2) + square),
    )


def solution(mesh):
    fine = Mesh(mesh.devices.reshape(XH, Z, CORE, Y, XL), TILE_AXES + ROW_AXES)
    placed = P(TILE_AXES, ROW_AXES, None, None)
    return jax.shard_map(
        body,
        mesh=fine,
        in_specs=(placed, P(), P(), P(), P(), placed),
        out_specs=(placed, placed, P(), P(), P()),
        check_vma=False,
    )
```
